32 devices in a mesh: groups: 2 (over x), pool: 2 (over core), tensor: 8 (over z, y).
Axes of the slice: x: 2, y: 2, z: 4, core: 2. Of those that a mesh axis runs over, the one named last changes fastest.
Arguments:
- hidden: bfloat16 [768, 8192], P('groups', ('pool', 'tensor')), parts along dimension 0, may hold values from -6 to 6
- norm_gain: float32 [8192], replicated, may hold values from 0.1 to 1.9
- w_query: bfloat16 [8192, 8192], P(None, ('pool', 'tensor')), may hold values from -0.0625 to 0.0625
- w_out: bfloat16 [8192, 8192], P(('pool', 'tensor')), may hold values from -1.5 to 1.5
- kv_pool: bfloat16 [64, 8, 2, 128, 128], P(('groups', 'pool', 'tensor')), parts along dimension 0
- draft_kv: bfloat16 [768, 2, 1024], P('groups'), parts along dimension 0, may hold values from -10 to 10
- block_table: int32 [8, 8], P('groups'), parts along dimension 0, may hold values from 0 to 31, as said below
- cached_len: int32 [8], P('groups'), parts along dimension 0, may hold values from 897 to 1024, as said below
- draft_pos: int32 [8, 96], P('groups'), parts along dimension 0, may hold values from 0 to 95, as said below
Outputs:
- attended: bfloat16 [768, 8192], P('groups'), parts along dimension 0
The draws below stay inside these ranges and needn't reach their ends.
There are 2 independent parts, one for each index of `groups`. The reference program is written for one: setup_inputs(seed, part) draws one part's arguments, and reference() takes and returns one part's arrays. A program takes and returns all parts, laid end to end along the dimension named above; an argument that names none is the same for every part. Nothing has to cross between parts.
Inputs may be any that keep to these rules, and one draw needn't show every extreme that they name: `block_table`: every pool block appears exactly once in the table. `cached_len`: each request's cached tokens end inside its last listed block; some request holds 1024 cached tokens. `draft_pos`: 0 for a request's first draft token, then rising by 0 or 1 from token to token; in some request it rises by 1 at every token.
All inputs are finite; a program needn't handle non-finite values.
Results may differ from the reference program's by a relative error of at most 0.006.
The reference program's roundings to bfloat16 on the way count: a program that leaves them out, or rounds other values in their place, can miss the bound.
Values may be sent and summed in bfloat16 or wider, within the bound.
A program may use at most 128 MiB of HBM per device.

```python
import jax
import jax.numpy as jnp
from jax import lax

D = 8192
HEADS = 64
KV_HEADS = 8
HEAD_DIM = 128
BLOCK = 128
REQS = 4
DRAFT = 96
POOL_BLOCKS = 32
MAX_BLOCKS = 8
TOK = 384


def draw_kv_pool(key, part):
    key = jax.random.fold_in(key, 11)
    base_key = jax.random.fold_in(key, 0)
    base = jax.random.normal(base_key, (POOL_BLOCKS, KV_HEADS, 2, BLOCK, HEAD_DIM), jnp.float32) * 1.5
    return base.astype(jnp.bfloat16)


def draw_block_table(key, part):
    key = jax.random.fold_in(key, 12)
    order = jax.random.permutation(key, POOL_BLOCKS)
    return order.reshape(REQS, MAX_BLOCKS).astype(jnp.int32)


def draw_cached_len(key, part):
    key = jax.random.fold_in(key, 13)
    length_key, pick_key = jax.random.split(key)
    lengths = jax.random.randint(length_key, (REQS,), (MAX_BLOCKS - 1) * BLOCK + 1, MAX_BLOCKS * BLOCK + 1)
    longest = jax.random.randint(pick_key, (), 0, REQS)
    lengths = jnp.where(jnp.arange(REQS) == longest, MAX_BLOCKS * BLOCK, lengths)
    return lengths.astype(jnp.int32)


def draw_draft_pos(key, part):
    key = jax.random.fold_in(key, 14)
    step_key, pick_key = jax.random.split(key)
    steps = jax.random.randint(step_key, (REQS, DRAFT), 0, 2)
    chosen = jax.random.randint(pick_key, (), 0, REQS)
    steps = jnp.where(jnp.arange(REQS)[:, None] == chosen, 1, steps)
    steps = jnp.where(jnp.arange(DRAFT)[None, :] == 0, 0, steps)
    return jnp.cumsum(steps, axis=1).astype(jnp.int32)


def levels(own_key, shape, shards, low, largest):
    factor_of, own = 1.0, jax.random.fold_in(own_key, 6)
    for axis_at, parts in shards:
        heights = jnp.exp(jax.random.uniform(jax.random.fold_in(own, axis_at), (parts,), jnp.float32, low / len(shards), largest / len(shards)))
        factor_of = factor_of * jnp.repeat(heights, shape[axis_at] // parts).reshape([-1 if axis == axis_at else 1 for axis in range(len(shape))])
    return factor_of


def bell_draw(rng, shape, width, reach, shards=(), kind=jnp.bfloat16):
    array = jax.random.normal(rng, shape, jnp.float32) * width
    if len(shards) > 0:
        array = levels(rng, shape, shards, -0.22, 0.18) * array
    return jnp.clip(array, min=-reach, max=reach).astype(kind)


def setup_inputs(seed: int = 0, part: int = 0) -> dict:
    key_of = jax.random.split(jax.random.key(seed), 10)
    own_keys = jax.random.split(jax.random.fold_in(key_of[9], part), 10)
    return {
        "hidden": bell_draw(own_keys[0], (TOK, D), 1.0, 6.0, ((1, 16),)),
        "norm_gain": jnp.clip(1.0 + 0.18 * jax.random.normal(key_of[1], (D,), jnp.float32), 0.1, 1.9),
        "w_query": bell_draw(key_of[2], (D, HEADS * HEAD_DIM), D ** -0.5, 0.0625, ((1, 16),)),
        "w_out": bell_draw(key_of[3], (HEADS * HEAD_DIM, D), 16 ** -0.5, 1.5, ((0, 16),)),
        "kv_pool": draw_kv_pool(jax.random.fold_in(jax.random.fold_in(key_of[9], part), 71), part),
        "draft_kv": bell_draw(own_keys[5], (TOK, 2, KV_HEADS * HEAD_DIM), 2.0, 10.0),
        "block_table": draw_block_table(jax.random.fold_in(jax.random.fold_in(key_of[9], part), 71), part),
        "cached_len": draw_cached_len(jax.random.fold_in(jax.random.fold_in(key_of[9], part), 71), part),
        "draft_pos": draw_draft_pos(jax.random.fold_in(jax.random.fold_in(key_of[9], part), 71), part),
    }


def rotate(values, positions):
    half_dim = values.shape[-1] // 2
    frequency = 500000.0 ** (-(jnp.arange(half_dim, dtype=jnp.float32) * 2.0) / values.shape[-1])
    angles = positions.astype(jnp.float32)[:, None] * frequency[None, :]
    cosine = jnp.cos(angles)[:, None, :]
    sine_part = jnp.sin(angles)[:, None, :]
    first_half = values[..., :half_dim]
    second_half = values[..., half_dim:]
    return jnp.concatenate([first_half * cosine - second_half * sine_part, second_half * cosine + first_half * sine_part], axis=-1)

def reference(hidden, norm_gain, w_query, w_out, kv_pool, draft_kv, block_table, cached_len, draft_pos):
    whole = hidden.astype(jnp.float32)
    normed_rows = (whole * lax.rsqrt(lax.optimization_barrier(jnp.mean(whole * whole, axis=-1, keepdims=True)) + 1e-05) * norm_gain).astype(jnp.bfloat16)
    raw_queries = jnp.dot(normed_rows, w_query, preferred_element_type=jnp.float32)
    positions = (cached_len[:, None] + draft_pos).reshape(-1)
    query_heads = (rotate(raw_queries.reshape(TOK, HEADS, HEAD_DIM), positions) * HEAD_DIM ** (-0.5)).astype(jnp.bfloat16)
    group_size = HEADS // KV_HEADS
    query_groups = query_heads.reshape(REQS, DRAFT, KV_HEADS, group_size, HEAD_DIM)
    draft_pairs = draft_kv.reshape(REQS, DRAFT, 2, KV_HEADS, HEAD_DIM)
    context = MAX_BLOCKS * BLOCK

    def one_request(items):
        queries, table_row, length, depth, pairs = items
        blocks = kv_pool[table_row].astype(jnp.float32)
        cache_keys = jnp.transpose(blocks[:, :, 0], (1, 0, 2, 3)).reshape(KV_HEADS, context, HEAD_DIM)
        cache_values = jnp.transpose(blocks[:, :, 1], (1, 0, 2, 3)).reshape(KV_HEADS, context, HEAD_DIM)
        query_wide = queries.astype(jnp.float32)
        cache_scores = jnp.einsum('qgjd,gkd->qgjk', query_wide, cache_keys, precision=lax.Precision.HIGHEST)
        cache_valid = jnp.arange(context) < length
        cache_scores = jnp.where(cache_valid[None, None, None, :], cache_scores, -jnp.inf)
        draft_keys = pairs[:, 0].astype(jnp.float32)
        draft_values = pairs[:, 1].astype(jnp.float32)
        draft_scores = jnp.einsum('qgjd,pgd->qgjp', query_wide, draft_keys, precision=lax.Precision.HIGHEST)
        draft_valid = (depth[None, :] < depth[:, None]) | jnp.eye(DRAFT, dtype=bool)
        draft_scores = jnp.where(draft_valid[:, None, None, :], draft_scores, -jnp.inf)
        row_peak = jnp.maximum(lax.optimization_barrier(jnp.max(cache_scores, axis=-1, keepdims=True)), lax.optimization_barrier(jnp.max(draft_scores, axis=-1, keepdims=True)))
        cache_weights = jnp.exp(cache_scores - row_peak)
        draft_weights = jnp.exp(draft_scores - row_peak)
        weight_sum = lax.optimization_barrier(jnp.sum(cache_weights, axis=-1, keepdims=True)) + lax.optimization_barrier(jnp.sum(draft_weights, axis=-1, keepdims=True))
        cache_probs = (cache_weights / weight_sum).astype(jnp.bfloat16).astype(jnp.float32)
        draft_probs = (draft_weights / weight_sum).astype(jnp.bfloat16).astype(jnp.float32)
        head_rows = jnp.einsum('qgjk,gkd->qgjd', cache_probs, cache_values, precision=lax.Precision.HIGHEST)
        head_rows = head_rows + jnp.einsum('qgjp,pgd->qgjd', draft_probs, draft_values, precision=lax.Precision.HIGHEST)
        return head_rows.astype(jnp.bfloat16).reshape(DRAFT, HEADS * HEAD_DIM)
    heads_out = lax.map(one_request, (query_groups, block_table, cached_len, draft_pos, draft_pairs))
    heads_out = heads_out.reshape(TOK, HEADS * HEAD_DIM)
    return jnp.dot(heads_out, w_out, preferred_element_type=jnp.float32).astype(jnp.bfloat16)
```

```python
import functools

import jax
import jax.numpy as jnp
from jax import lax
from jax.experimental import pallas as pl
from jax.experimental.pallas import tpu as pltpu
from jax.sharding import PartitionSpec as P

VMEM_LIMIT = 56 * 1024 * 1024


def rotate(values, positions):
    half_dim = values.shape[-1] // 2
    frequency = 500000.0 ** (-(jnp.arange(half_dim, dtype=jnp.float32) * 2.0) / values.shape[-1])
    angles = positions.astype(jnp.float32)[:, None] * frequency[None, :]
    cosine = jnp.cos(angles)[:, None, :]
    sine_part = jnp.sin(angles)[:, None, :]
    first_half = values[..., :half_dim]
    second_half = values[..., half_dim:]
    return jnp.concatenate(
        [
            first_half * cosine - second_half * sine_part,
            second_half * cosine + first_half * sine_part,
        ],
        axis=-1,
    )


class Place:
    def __init__(self, ny, nt):
        self.ny, self.nz, self.nt = ny, nt // ny, nt
        self.p = lax.axis_index("pool")
        self.t = lax.axis_index("tensor")
        self.y = lax.rem(self.t, ny)
        self.z = self.t // ny

    def chip(self, z, y):
        return z * self.ny + y

    def up(self, z, by):
        return lax.rem(z + by, self.nz)

    def down(self, z, by):
        return lax.rem(z + self.nz - by, self.nz)

    def rank(self, p, t):
        return p * self.nt + t

    @property
    def mate(self):
        return {"pool": 1 - self.p, "tensor": self.t}

    @property
    def across(self):
        return {"pool": self.p, "tensor": self.chip(self.z, 1 - self.y)}

    @property
    def next(self):
        return {"pool": self.p, "tensor": self.chip(self.up(self.z, 1), self.y)}

    @property
    def previous(self):
        return {"pool": self.p, "tensor": self.chip(self.down(self.z, 1), self.y)}


def remote(src, dst, send, recv, device):
    return pltpu.make_async_remote_copy(
        src_ref=src,
        dst_ref=dst,
        send_sem=send,
        recv_sem=recv,
        device_id=device,
        device_id_type=pl.DeviceIdType.MESH,
    )


def meet(devices):
    barrier = pltpu.get_barrier_semaphore()
    for device in devices:
        pl.semaphore_signal(barrier, inc=1, device_id=device, device_id_type=pl.DeviceIdType.MESH)
    pl.semaphore_wait(barrier, len(devices))


def gather_columns(at, own, out, width, sems):
    zs, zr, ys, yr, ms, mr, ls = sems
    nz, ny = at.nz, at.ny

    def block(p, z, y):
        start = pl.multiple_of(at.rank(p, at.chip(z, y)) * width, width)
        return out.at[:, pl.ds(start, width)]

    keep = pltpu.make_async_copy(own, block(at.p, at.z, at.y), ls)
    keep.start()
    started = []

    def ring(s):
        z = at.down(at.z, s)
        here = block(at.p, z, at.y)
        src = own if s == 0 else here
        if s > 0:
            remote(here, here, zs.at[s - 1], zr.at[s - 1], at.previous).wait_recv()
        if s < nz - 1:
            started.append(remote(src, here, zs.at[s], zr.at[s], at.next))
            started[-1].start()
        if ny == 2:
            started.append(remote(src, here, ys.at[s], yr.at[s], at.across))
            started[-1].start()
        started.append(remote(src, here, ms.at[s], mr.at[s], at.mate))
        started[-1].start()

    def from_across(s):
        if ny == 2:
            there = block(at.p, at.down(at.z, s), 1 - at.y)
            remote(there, there, ys.at[s], yr.at[s], at.across).wait_recv()
            started.append(remote(there, there, ms.at[nz + s], mr.at[nz + s], at.mate))
            started[-1].start()

    def finish():
        for s in range(nz):
            z = at.down(at.z, s)
            for y_at in range(ny):
                y = at.y if y_at == 0 else 1 - at.y
                there = block(1 - at.p, z, y)
                slot = s + y_at * nz
                remote(there, there, ms.at[slot], mr.at[slot], at.mate).wait_recv()
        for copy in started:
            copy.wait_send()
        keep.wait()

    return ring, from_across, finish


def gather_sems(ny, nz):
    dma = pltpu.SemaphoreType.DMA
    return [dma((nz,)), dma((nz,)), dma((nz,)), dma((nz,)), dma((2 * nz,)), dma((2 * nz,)), dma]


def front_kernel(
    ny, nt, group_size, hidden, kv, w_out, whole, blocks, w_mate,
    zs, zr, ys, yr, ms, mr, ls, ks, kr, fs, fr, ws, wr, bs,
):
    at = Place(ny, nt)
    nz = at.nz
    others = []
    for dz in range(nz):
        for dp in range(2):
            if dz + dp > 0:
                q = lax.rem(at.p + dp, 2)
                others.append({"pool": q, "tensor": at.chip(at.up(at.z, dz), at.y)})
    meet(others + ([at.across] if ny == 2 else []))

    width = hidden.shape[1]
    ring, from_across, finish = gather_columns(
        at, hidden, whole, width, (zs, zr, ys, yr, ms, mr, ls)
    )
    ring(0)
    me = at.rank(at.p, at.t)

    def head_of(p, t):
        return at.rank(p, t) // group_size

    keep = pltpu.make_async_copy(kv.at[:, head_of(at.p, at.t)], blocks.at[me], bs)
    keep.start()
    half = w_mate.shape[1]
    swap = remote(
        w_out.at[:, pl.ds(pl.multiple_of((1 - at.p) * half, half), half)],
        w_mate, ws, wr, at.mate,
    )
    sends = []
    index = 0
    for dz in range(nz):
        for dp in range(2):
            if dz + dp > 0:
                device = others[index]
                index += 1
                slot = dz * 2 + dp
                head = head_of(device["pool"], device["tensor"])
                sends.append(remote(kv.at[:, head], blocks.at[me], ks.at[slot], kr.at[slot], device))
                sends[-1].start()
    swap.start()

    def block_from(dz, dp):
        return at.rank(lax.rem(at.p + dp, 2), at.chip(at.down(at.z, dz), at.y))

    def forward(dz):
        for dp in range(2):
            slot = dz * 2 + dp
            here = blocks.at[block_from(dz, dp)]
            src = here
            if slot == 0:
                src = kv.at[:, head_of(at.p, at.t)]
            else:
                remote(here, here, ks.at[slot], kr.at[slot], at.mate).wait_recv()
            if ny == 2:
                sends.append(remote(src, here, fs.at[slot], fr.at[slot], at.across))
                sends[-1].start()

    forward(0)
    for s in range(1, nz):
        ring(s)
        from_across(s - 1)
        forward(s)
    from_across(nz - 1)
    finish()
    if ny == 2:
        for dz in range(nz):
            for dp in range(2):
                slot = dz * 2 + dp
                source = at.rank(
                    lax.rem(at.p + dp, 2), at.chip(at.down(at.z, dz), 1 - at.y)
                )
                there = blocks.at[source]
                remote(there, there, fs.at[slot], fr.at[slot], at.across).wait_recv()
    for copy in sends:
        copy.wait_send()
    swap.wait()
    keep.wait()


def front(ny, nt, group_size, hidden, kv_pool, w_out):
    rows, width = hidden.shape
    nz = nt // ny
    dma = pltpu.SemaphoreType.DMA
    blocks = (2 * nt, kv_pool.shape[0]) + kv_pool.shape[2:]
    return pl.pallas_call(
        functools.partial(front_kernel, ny, nt, group_size),
        out_shape=(
            jax.ShapeDtypeStruct((rows, width * 2 * nt), hidden.dtype),
            jax.ShapeDtypeStruct(blocks, kv_pool.dtype),
            jax.ShapeDtypeStruct((w_out.shape[0], w_out.shape[1] // 2), w_out.dtype),
        ),
        in_specs=[pl.BlockSpec(memory_space=pl.ANY)] * 3,
        out_specs=(pl.BlockSpec(memory_space=pl.ANY),) * 3,
        scratch_shapes=gather_sems(ny, nz)
        + [dma((2 * nz,)), dma((2 * nz,)), dma((2 * nz,)), dma((2 * nz,)), dma, dma, dma],
        compiler_params=pltpu.CompilerParams(
            collective_id=0, has_side_effects=True, vmem_limit_bytes=VMEM_LIMIT
        ),
        name="front",
    )(hidden, kv_pool, w_out)


def back_kernel(
    ny, nt, heads, w_own, w_mate, out,
    heads_mate, w_buf, y_send, y_recv, z_send, z_recv, final,
    hs, hr, w_sem, ps, pr, qs, qr, zs, zr, ys, yr, ms, mr, ls,
):
    at = Place(ny, nt)
    nz = at.nz
    width = final.shape[1]
    half = w_mate.shape[1]

    def load(which, t):
        if which == 0:
            start = pl.multiple_of(at.p * half + t * width, width)
            src = w_own.at[:, pl.ds(start, width)]
        else:
            src = w_mate.at[:, pl.ds(pl.multiple_of(t * width, width), width)]
        return pltpu.make_async_copy(src, w_buf.at[which, t], w_sem.at[which, t])

    def chunk(s):
        return at.down(at.z, s + 1)

    def chip_of(s, y):
        return at.chip(lax.rem(at.z + 2 * nz - 1 - s, nz), y)

    def start_loads(y):
        def body(s, carry):
            t = chip_of(s, y)
            load(0, t).start()
            load(1, t).start()
            return carry

        lax.fori_loop(0, nz, body, 0)

    if ny == 2:
        start_loads(1 - at.y)
    start_loads(at.y)
    neighbours = [at.mate, at.next, at.previous] + ([at.across] if ny == 2 else [])
    meet(neighbours)
    trade = remote(heads, heads_mate, hs, hr, at.mate)
    trade.start()
    trade.wait()

    def term(t):
        load(0, t).wait()
        load(1, t).wait()
        return jnp.dot(heads[...], w_buf[0, t], preferred_element_type=jnp.float32) + jnp.dot(
            heads_mate[...], w_buf[1, t], preferred_element_type=jnp.float32
        )

    def across_copy(s):
        return remote(y_send.at[s], y_recv.at[s], ps.at[s], pr.at[s], at.across)

    def ring_copy(s):
        return remote(z_send.at[s], z_recv.at[s], qs.at[s], qr.at[s], at.next)

    if ny == 2:

        def send_across(s, carry):
            y_send[s] = term(chip_of(s, 1 - at.y))
            across_copy(s).start()
            return carry

        lax.fori_loop(0, nz, send_across, 0)

    def total(s):
        value = term(chip_of(s, at.y))
        if ny == 2:
            across_copy(s).wait_recv()
            value = value + y_recv[s]
        return value

    z_send[0] = total(0)
    ring_copy(0).start()

    def ring_step(s, carry):
        value = total(s)
        ring_copy(s - 1).wait_recv()
        z_send[s] = value + z_recv[s - 1]
        ring_copy(s).start()
        return carry

    lax.fori_loop(1, nz - 1, ring_step, 0)
    value = total(nz - 1)
    ring_copy(nz - 2).wait_recv()
    final[...] = (value + z_recv[nz - 2]).astype(final.dtype)

    ring, from_across, finish = gather_columns(
        at, final, out, width, (zs, zr, ys, yr, ms, mr, ls)
    )
    ring(0)
    for s in range(1, nz):
        ring(s)
        from_across(s - 1)
    from_across(nz - 1)
    finish()

    def sent(s, carry):
        if ny == 2:
            across_copy(s).wait_send()
        return carry

    lax.fori_loop(0, nz, sent, 0)

    def ring_sent(s, carry):
        ring_copy(s).wait_send()
        return carry

    lax.fori_loop(0, nz - 1, ring_sent, 0)


def back(ny, nt, heads, w_out, w_mate):
    rows, depth = heads.shape
    columns = w_out.shape[1]
    nz = nt // ny
    width = columns // (2 * nt)
    dma = pltpu.SemaphoreType.DMA
    f32 = jnp.float32
    return pl.pallas_call(
        functools.partial(back_kernel, ny, nt),
        out_shape=jax.ShapeDtypeStruct((rows, columns), jnp.bfloat16),
        in_specs=[
            pl.BlockSpec(memory_space=pltpu.VMEM),
            pl.BlockSpec(memory_space=pl.ANY),
            pl.BlockSpec(memory_space=pl.ANY),
        ],
        out_specs=pl.BlockSpec(memory_space=pl.ANY),
        scratch_shapes=[
            pltpu.VMEM((rows, depth), heads.dtype),
            pltpu.VMEM((2, nt, depth, width), w_out.dtype),
            pltpu.VMEM((nz, rows, width), f32),
            pltpu.VMEM((nz, rows, width), f32),
            pltpu.VMEM((nz - 1, rows, width), f32),
            pltpu.VMEM((nz - 1, rows, width), f32),
            pltpu.VMEM((rows, width), jnp.bfloat16),
            dma,
            dma,
            dma((2, nt)),
            dma((nz,)),
            dma((nz,)),
            dma((nz,)),
            dma((nz,)),
        ]
        + gather_sems(ny, nz),
        compiler_params=pltpu.CompilerParams(
            collective_id=1, has_side_effects=True, vmem_limit_bytes=VMEM_LIMIT
        ),
        name="back",
    )(heads, w_out, w_mate)


def shards(
    hidden, norm_gain, w_query, w_out, kv_pool, draft_kv, block_table, cached_len, draft_pos
):
    nt = lax.axis_size("tensor")
    ny = 2 if nt == 8 else 1
    devices = lax.axis_size(("pool", "tensor"))
    my_rank = lax.axis_index(("pool", "tensor"))
    kv_heads = kv_pool.shape[1]
    block_len = kv_pool.shape[3]
    head_dim = kv_pool.shape[4]
    requests = draft_pos.shape[0]
    drafts = draft_pos.shape[1]
    listed = block_table.shape[1]
    context = listed * block_len
    local_heads = w_query.shape[1] // head_dim
    group_size = devices // kv_heads
    own_head = my_rank // group_size
    gathered, arrived, w_mate = front(ny, nt, group_size, hidden, kv_pool, w_out)
    whole = gathered.astype(jnp.float32)
    normed_rows = (
        whole * lax.rsqrt(jnp.mean(whole * whole, axis=-1, keepdims=True) + 1e-05) * norm_gain
    ).astype(jnp.bfloat16)
    raw_queries = jnp.dot(normed_rows, w_query, preferred_element_type=jnp.float32)
    positions = (cached_len[:, None] + draft_pos).reshape(-1)
    query_heads = (
        rotate(raw_queries.reshape(-1, local_heads, head_dim), positions) * head_dim ** (-0.5)
    ).astype(jnp.bfloat16)
    query_heads = query_heads.reshape(requests, drafts, local_heads, head_dim)
    own_draft = lax.dynamic_slice_in_dim(draft_kv, own_head * head_dim, head_dim, axis=2)
    own_draft = own_draft.reshape(requests, drafts, 2, head_dim)
    draft_keys = own_draft[:, :, 0]
    draft_values = own_draft[:, :, 1]
    draft_valid = (draft_pos[:, None, :] < draft_pos[:, :, None]) | jnp.eye(drafts, dtype=bool)[
        None
    ]
    arrived = arrived.reshape(-1, 2, block_len, head_dim)
    gathered_blocks = arrived[block_table]
    cache_keys = gathered_blocks[:, :, 0].reshape(requests, context, head_dim)
    cache_values = gathered_blocks[:, :, 1].reshape(requests, context, head_dim)
    cache_scores = jnp.einsum(
        "rqhd,rkd->rqhk", query_heads, cache_keys, preferred_element_type=jnp.float32
    )
    cache_valid = jnp.arange(context)[None, :] < cached_len[:, None]
    cache_scores = jnp.where(cache_valid[:, None, None, :], cache_scores, -jnp.inf)
    draft_scores = jnp.einsum(
        "rqhd,rpd->rqhp", query_heads, draft_keys, preferred_element_type=jnp.float32
    )
    draft_scores = jnp.where(draft_valid[:, :, None, :], draft_scores, -jnp.inf)
    row_peak = jnp.maximum(
        jnp.max(cache_scores, axis=-1, keepdims=True), jnp.max(draft_scores, axis=-1, keepdims=True)
    )
    cache_weights = jnp.exp(cache_scores - row_peak)
    draft_weights = jnp.exp(draft_scores - row_peak)
    weight_sum = jnp.sum(cache_weights, axis=-1, keepdims=True) + jnp.sum(
        draft_weights, axis=-1, keepdims=True
    )
    cache_probs = (cache_weights / weight_sum).astype(jnp.bfloat16)
    draft_probs = (draft_weights / weight_sum).astype(jnp.bfloat16)
    head_rows = jnp.einsum(
        "rqhk,rkd->rqhd", cache_probs, cache_values, preferred_element_type=jnp.float32
    )
    head_rows = head_rows + jnp.einsum(
        "rqhp,rpd->rqhd", draft_probs, draft_values, preferred_element_type=jnp.float32
    )
    heads_out = head_rows.astype(jnp.bfloat16).reshape(requests * drafts, local_heads * head_dim)
    return back(ny, nt, heads_out, w_out, w_mate)


def solution(mesh):
    placed = (
        P("groups", ("pool", "tensor")),
        P(),
        P(None, ("pool", "tensor")),
        P(("pool", "tensor"), None),
        P(("groups", "pool", "tensor"), None, None, None, None),
        P("groups", None, None),
        P("groups", None),
        P("groups"),
        P("groups", None),
    )
    return jax.shard_map(
        shards, mesh=mesh, in_specs=placed, out_specs=P("groups", None), check_vma=False
    )
```

```python
import functools

import jax
import jax.numpy as jnp
from jax import lax
from jax.experimental import pallas as pl
from jax.experimental.pallas import tpu as pltpu
from jax.sharding import PartitionSpec as P

VMEM_LIMIT = 56 * 1024 * 1024


def rotate(values, positions):
    half_dim = values.shape[-1] // 2
    frequency = 500000.0 ** (-(jnp.arange(half_dim, dtype=jnp.float32) * 2.0) / values.shape[-1])
    angles = positions.astype(jnp.float32)[:, None] * frequency[None, :]
    cosine = jnp.cos(angles)[:, None, :]
    sine_part = jnp.sin(angles)[:, None, :]
    first_half = values[..., :half_dim]
    second_half = values[..., half_dim:]
    return jnp.concatenate(
        [
            first_half * cosine - second_half * sine_part,
            second_half * cosine + first_half * sine_part,
        ],
        axis=-1,
    )


class Place:
    def __init__(self, ny, nt):
        self.ny, self.nz, self.nt = ny, nt // ny, nt
        self.p = lax.axis_index("pool")
        self.t = lax.axis_index("tensor")
        self.y = lax.rem(self.t, ny)
        self.z = self.t // ny

    def chip(self, z, y):
        return z * self.ny + y

    def up(self, z, by):
        return lax.rem(z + by, self.nz)

    def down(self, z, by):
        return lax.rem(z + self.nz - by, self.nz)

    def rank(self, p, t):
        return p * self.nt + t

    @property
    def mate(self):
        return {"pool": 1 - self.p, "tensor": self.t}

    @property
    def across(self):
        return {"pool": self.p, "tensor": self.chip(self.z, 1 - self.y)}

    @property
    def next(self):
        return {"pool": self.p, "tensor": self.chip(self.up(self.z, 1), self.y)}

    @property
    def previous(self):
        return {"pool": self.p, "tensor": self.chip(self.down(self.z, 1), self.y)}


def remote(src, dst, send, recv, device):
    return pltpu.make_async_remote_copy(
        src_ref=src,
        dst_ref=dst,
        send_sem=send,
        recv_sem=recv,
        device_id=device,
        device_id_type=pl.DeviceIdType.MESH,
    )


def meet(devices):
    barrier = pltpu.get_barrier_semaphore()
    for device in devices:
        pl.semaphore_signal(barrier, inc=1, device_id=device, device_id_type=pl.DeviceIdType.MESH)
    pl.semaphore_wait(barrier, len(devices))


def gather_blocks(at, own, block_of, sems, use=None):
    zs, zr, ys, yr, ms, mr, ls = sems
    nz, ny = at.nz, at.ny

    def block(p, z, y):
        return block_of(at.rank(p, at.chip(z, y)))

    keep = None
    if use is None:
        keep = pltpu.make_async_copy(own, block(at.p, at.z, at.y), ls)
        keep.start()
    started = []

    def ring(s):
        z = at.down(at.z, s)
        here = block(at.p, z, at.y)
        src = own if s == 0 else here
        if s > 0:
            remote(here, here, zs.at[s - 1], zr.at[s - 1], at.previous).wait_recv()
        if s < nz - 1:
            started.append(remote(src, here, zs.at[s], zr.at[s], at.next))
            started[-1].start()
        if ny == 2:
            started.append(remote(src, here, ys.at[s], yr.at[s], at.across))
            started[-1].start()
        started.append(remote(src, here, ms.at[s], mr.at[s], at.mate))
        started[-1].start()

    def from_across(s):
        if ny == 2:
            there = block(at.p, at.down(at.z, s), 1 - at.y)
            remote(there, there, ys.at[s], yr.at[s], at.across).wait_recv()
            started.append(remote(there, there, ms.at[nz + s], mr.at[nz + s], at.mate))
            started[-1].start()

    def arrive(s):
        z = at.down(at.z, s)
        for y_at in range(ny):
            y = at.y if y_at == 0 else 1 - at.y
            there = block(1 - at.p, z, y)
            slot = s + y_at * nz
            if use is not None and s + y_at > 0:
                use(at.rank(at.p, at.chip(z, y)))
            remote(there, there, ms.at[slot], mr.at[slot], at.mate).wait_recv()
            if use is not None:
                use(at.rank(1 - at.p, at.chip(z, y)))

    def finish():
        for copy in started:
            copy.wait_send()
        if keep is not None:
            keep.wait()

    return ring, from_across, arrive, finish


def gather_sems(ny, nz):
    dma = pltpu.SemaphoreType.DMA
    return [dma((nz,)), dma((nz,)), dma((nz,)), dma((nz,)), dma((2 * nz,)), dma((2 * nz,)), dma]


def front_kernel(
    ny, nt, group_size, hidden, gain, kv, w_out, w_query, raw, blocks, w_mate,
    squares, squares_all, normed, gathered, w_buf,
    zs, zr, ys, yr, ms, mr, ls, ks, kr, fs, fr, ws, wr, bs, w_sem, ss, sr,
):
    at = Place(ny, nt)
    nz = at.nz
    ranks = 2 * nt
    width = hidden.shape[1]

    def load(rank):
        start = pl.multiple_of(rank * width, width)
        return pltpu.make_async_copy(
            w_query.at[pl.ds(start, width), :], w_buf.at[rank], w_sem.at[rank]
        )

    def start_load(rank, carry):
        load(rank).start()
        return carry

    lax.fori_loop(0, ranks, start_load, 0)
    others = []
    for dt in range(nt):
        for dp in range(2):
            if dt + dp > 0:
                others.append({"pool": lax.rem(at.p + dp, 2), "tensor": lax.rem(at.t + dt, nt)})
    meet(others)
    me = at.rank(at.p, at.t)

    wide = hidden[...].astype(jnp.float32)
    squares[...] = lax.dot_general(
        jnp.ones((8, width), jnp.float32), wide * wide, (((1,), (1,)), ((), ())),
        precision=lax.Precision.HIGHEST, preferred_element_type=jnp.float32,
    )
    square_copies = [
        remote(squares, squares_all.at[i], ss.at[i], sr.at[i], device)
        for i, device in enumerate(others)
    ]
    for copy in square_copies:
        copy.start()

    def head_of(p, t):
        return at.rank(p, t) // group_size

    keep = pltpu.make_async_copy(kv.at[:, head_of(at.p, at.t)], blocks.at[me], bs)
    keep.start()
    half = w_mate.shape[1]
    swap = remote(
        w_out.at[:, pl.ds(pl.multiple_of((1 - at.p) * half, half), half)],
        w_mate, ws, wr, at.mate,
    )
    sends = []
    for dz in range(nz):
        for dp in range(2):
            if dz + dp > 0:
                device = {
                    "pool": lax.rem(at.p + dp, 2),
                    "tensor": at.chip(at.up(at.z, dz), at.y),
                }
                slot = dz * 2 + dp
                head = head_of(device["pool"], device["tensor"])
                sends.append(remote(kv.at[:, head], blocks.at[me], ks.at[slot], kr.at[slot], device))
                sends[-1].start()

    total = squares[...]
    for i, copy in enumerate(square_copies):
        copy.wait_recv()
        total = total + squares_all[i]
    scale = lax.rsqrt(total * (1.0 / (width * ranks)) + 1e-05)
    scale = jnp.transpose(jnp.concatenate([scale] * 16, axis=0))
    for c in range(width // 128):
        lanes = slice(c * 128, (c + 1) * 128)
        normed[:, lanes] = (
            hidden[:, lanes].astype(jnp.float32) * scale * gain[:, lanes]
        ).astype(normed.dtype)

    def use(rank):
        load(rank).wait()
        raw[...] += jnp.dot(gathered[rank], w_buf[rank], preferred_element_type=jnp.float32)

    ring, from_across, arrive, finish = gather_blocks(
        at, normed, lambda rank: gathered.at[rank], (zs, zr, ys, yr, ms, mr, ls), use
    )

    def block_from(dz, dp):
        return at.rank(lax.rem(at.p + dp, 2), at.chip(at.down(at.z, dz), at.y))

    def forward(dz):
        for dp in range(2):
            slot = dz * 2 + dp
            here = blocks.at[block_from(dz, dp)]
            src = here
            if slot == 0:
                src = kv.at[:, head_of(at.p, at.t)]
            else:
                remote(here, here, ks.at[slot], kr.at[slot], at.mate).wait_recv()
            if ny == 2:
                sends.append(remote(src, here, fs.at[slot], fr.at[slot], at.across))
                sends[-1].start()

    ring(0)
    forward(0)
    swap.start()
    load(me).wait()
    raw[...] = jnp.dot(normed[...], w_buf[me], preferred_element_type=jnp.float32)
    for s in range(1, nz):
        ring(s)
        from_across(s - 1)
        forward(s)
        arrive(s - 1)
    from_across(nz - 1)
    arrive(nz - 1)
    finish()
    if ny == 2:
        for dz in range(nz):
            for dp in range(2):
                slot = dz * 2 + dp
                source = at.rank(
                    lax.rem(at.p + dp, 2), at.chip(at.down(at.z, dz), 1 - at.y)
                )
                there = blocks.at[source]
                remote(there, there, fs.at[slot], fr.at[slot], at.across).wait_recv()
    for copy in sends + square_copies:
        copy.wait_send()
    swap.wait()
    keep.wait()


def front(ny, nt, group_size, hidden, gain, kv_pool, w_out, w_query):
    rows, width = hidden.shape
    columns = w_query.shape[1]
    nz = nt // ny
    ranks = 2 * nt
    dma = pltpu.SemaphoreType.DMA
    blocks = (ranks, kv_pool.shape[0]) + kv_pool.shape[2:]
    return pl.pallas_call(
        functools.partial(front_kernel, ny, nt, group_size),
        out_shape=(
            jax.ShapeDtypeStruct((rows, columns), jnp.float32),
            jax.ShapeDtypeStruct(blocks, kv_pool.dtype),
            jax.ShapeDtypeStruct((w_out.shape[0], w_out.shape[1] // 2), w_out.dtype),
        ),
        in_specs=[pl.BlockSpec(memory_space=pltpu.VMEM)] * 2
        + [pl.BlockSpec(memory_space=pl.ANY)] * 3,
        out_specs=(
            pl.BlockSpec(memory_space=pltpu.VMEM),
            pl.BlockSpec(memory_space=pl.ANY),
            pl.BlockSpec(memory_space=pl.ANY),
        ),
        scratch_shapes=[
            pltpu.VMEM((8, rows), jnp.float32),
            pltpu.VMEM((ranks - 1, 8, rows), jnp.float32),
            pltpu.VMEM((rows, width), hidden.dtype),
            pltpu.VMEM((ranks, rows, width), hidden.dtype),
            pltpu.VMEM((ranks, width, columns), w_query.dtype),
        ]
        + gather_sems(ny, nz)
        + [dma((2 * nz,)), dma((2 * nz,)), dma((2 * nz,)), dma((2 * nz,)), dma, dma, dma]
        + [dma((ranks,)), dma((ranks - 1,)), dma((ranks - 1,))],
        compiler_params=pltpu.CompilerParams(
            collective_id=0, has_side_effects=True, vmem_limit_bytes=VMEM_LIMIT
        ),
        name="front",
    )(hidden, gain, kv_pool, w_out, w_query)


def code(value, codes, scales):
    peak = jnp.maximum(jnp.max(jnp.abs(value), axis=0, keepdims=True), 1e-30)
    codes[...] = jnp.round(value * (32767.0 / peak)).astype(jnp.int32).astype(jnp.int16)
    scales[...] = jnp.broadcast_to(peak * (1.0 / 32767.0), scales.shape)


def decode(codes, scales):
    return codes[...].astype(jnp.int32).astype(jnp.float32) * scales[0:1, :]


def back_kernel(
    ny, nt, heads, w_own, w_mate, out,
    heads_mate, w_buf, y_send, y_recv, z_send, z_recv,
    y_send_scale, y_recv_scale, z_send_scale, z_recv_scale, final,
    hs, hr, w_sem, ps, pr, qs, qr, pss, psr, qss, qsr, zs, zr, ys, yr, ms, mr, ls,
):
    at = Place(ny, nt)
    nz = at.nz
    width = final.shape[1]
    half = w_mate.shape[1]

    def load(which, t):
        if which == 0:
            start = pl.multiple_of(at.p * half + t * width, width)
            src = w_own.at[:, pl.ds(start, width)]
        else:
            src = w_mate.at[:, pl.ds(pl.multiple_of(t * width, width), width)]
        return pltpu.make_async_copy(src, w_buf.at[which, t], w_sem.at[which, t])

    def chunk(s):
        return at.down(at.z, s + 1)

    def chip_of(s, y):
        return at.chip(lax.rem(at.z + 2 * nz - 1 - s, nz), y)

    def start_loads(y):
        def body(s, carry):
            t = chip_of(s, y)
            load(0, t).start()
            load(1, t).start()
            return carry

        lax.fori_loop(0, nz, body, 0)

    if ny == 2:
        start_loads(1 - at.y)
    start_loads(at.y)
    neighbours = [at.mate, at.next, at.previous] + ([at.across] if ny == 2 else [])
    meet(neighbours)
    trade = remote(heads, heads_mate, hs, hr, at.mate)
    trade.start()
    trade.wait()

    def term(t):
        load(0, t).wait()
        load(1, t).wait()
        return jnp.dot(heads[...], w_buf[0, t], preferred_element_type=jnp.float32) + jnp.dot(
            heads_mate[...], w_buf[1, t], preferred_element_type=jnp.float32
        )

    def across_copies(s):
        return [
            remote(y_send.at[s], y_recv.at[s], ps.at[s], pr.at[s], at.across),
            remote(y_send_scale.at[s], y_recv_scale.at[s], pss.at[s], psr.at[s], at.across),
        ]

    def ring_copies(s):
        return [
            remote(z_send.at[s], z_recv.at[s], qs.at[s], qr.at[s], at.next),
            remote(z_send_scale.at[s], z_recv_scale.at[s], qss.at[s], qsr.at[s], at.next),
        ]

    if ny == 2:

        def send_across(s, carry):
            code(term(chip_of(s, 1 - at.y)), y_send.at[s], y_send_scale.at[s])
            for copy in across_copies(s):
                copy.start()
            return carry

        lax.fori_loop(0, nz, send_across, 0)

    def total(s):
        value = term(chip_of(s, at.y))
        if ny == 2:
            for copy in across_copies(s):
                copy.wait_recv()
            value = value + decode(y_recv.at[s], y_recv_scale.at[s])
        return value

    def ring_received(s):
        for copy in ring_copies(s):
            copy.wait_recv()
        return decode(z_recv.at[s], z_recv_scale.at[s])

    def ring_send(s, value):
        code(value, z_send.at[s], z_send_scale.at[s])
        for copy in ring_copies(s):
            copy.start()

    ring_send(0, total(0))

    def ring_step(s, carry):
        value = total(s)
        ring_send(s, value + ring_received(s - 1))
        return carry

    lax.fori_loop(1, nz - 1, ring_step, 0)
    value = total(nz - 1)
    final[...] = (value + ring_received(nz - 2)).astype(final.dtype)

    def block_of(rank):
        return out.at[:, pl.ds(pl.multiple_of(rank * width, width), width)]

    ring, from_across, arrive, finish = gather_blocks(
        at, final, block_of, (zs, zr, ys, yr, ms, mr, ls)
    )
    ring(0)
    for s in range(1, nz):
        ring(s)
        from_across(s - 1)
    from_across(nz - 1)
    for s in range(nz):
        arrive(s)
    finish()

    def sent(s, carry):
        if ny == 2:
            for copy in across_copies(s):
                copy.wait_send()
        return carry

    lax.fori_loop(0, nz, sent, 0)

    def ring_sent(s, carry):
        for copy in ring_copies(s):
            copy.wait_send()
        return carry

    lax.fori_loop(0, nz - 1, ring_sent, 0)


def back(ny, nt, heads, w_out, w_mate):
    rows, depth = heads.shape
    columns = w_out.shape[1]
    nz = nt // ny
    width = columns // (2 * nt)
    dma = pltpu.SemaphoreType.DMA
    f32 = jnp.float32
    return pl.pallas_call(
        functools.partial(back_kernel, ny, nt),
        out_shape=jax.ShapeDtypeStruct((rows, columns), jnp.bfloat16),
        in_specs=[
            pl.BlockSpec(memory_space=pltpu.VMEM),
            pl.BlockSpec(memory_space=pl.ANY),
            pl.BlockSpec(memory_space=pl.ANY),
        ],
        out_specs=pl.BlockSpec(memory_space=pl.ANY),
        scratch_shapes=[
            pltpu.VMEM((rows, depth), heads.dtype),
            pltpu.VMEM((2, nt, depth, width), w_out.dtype),
            pltpu.VMEM((nz, rows, width), jnp.int16),
            pltpu.VMEM((nz, rows, width), jnp.int16),
            pltpu.VMEM((nz - 1, rows, width), jnp.int16),
            pltpu.VMEM((nz - 1, rows, width), jnp.int16),
            pltpu.VMEM((nz, 8, width), f32),
            pltpu.VMEM((nz, 8, width), f32),
            pltpu.VMEM((nz - 1, 8, width), f32),
            pltpu.VMEM((nz - 1, 8, width), f32),
            pltpu.VMEM((rows, width), jnp.bfloat16),
            dma,
            dma,
            dma((2, nt)),
            dma((nz,)),
            dma((nz,)),
            dma((nz,)),
            dma((nz,)),
            dma((nz,)),
            dma((nz,)),
            dma((nz,)),
            dma((nz,)),
        ]
        + gather_sems(ny, nz),
        compiler_params=pltpu.CompilerParams(
            collective_id=1, has_side_effects=True, vmem_limit_bytes=VMEM_LIMIT
        ),
        name="back",
    )(heads, w_out, w_mate)


def shards(
    hidden, norm_gain, w_query, w_out, kv_pool, draft_kv, block_table, cached_len, draft_pos
):
    nt = lax.axis_size("tensor")
    ny = 2 if nt == 8 else 1
    devices = lax.axis_size(("pool", "tensor"))
    my_rank = lax.axis_index(("pool", "tensor"))
    kv_heads = kv_pool.shape[1]
    block_len = kv_pool.shape[3]
    head_dim = kv_pool.shape[4]
    requests = draft_pos.shape[0]
    drafts = draft_pos.shape[1]
    listed = block_table.shape[1]
    context = listed * block_len
    local_heads = w_query.shape[1] // head_dim
    group_size = devices // kv_heads
    own_head = my_rank // group_size
    width = hidden.shape[1]
    gain = lax.dynamic_slice_in_dim(norm_gain, my_rank * width, width).reshape(1, width)
    raw_queries, arrived, w_mate = front(
        ny, nt, group_size, hidden, gain, kv_pool, w_out, w_query
    )
    positions = (cached_len[:, None] + draft_pos).reshape(-1)
    query_heads = (
        rotate(raw_queries.reshape(-1, local_heads, head_dim), positions) * head_dim ** (-0.5)
    ).astype(jnp.bfloat16)
    query_heads = query_heads.reshape(requests, drafts, local_heads, head_dim)
    own_draft = lax.dynamic_slice_in_dim(draft_kv, own_head * head_dim, head_dim, axis=2)
    own_draft = own_draft.reshape(requests, drafts, 2, head_dim)
    draft_keys = own_draft[:, :, 0]
    draft_values = own_draft[:, :, 1]
    draft_valid = (draft_pos[:, None, :] < draft_pos[:, :, None]) | jnp.eye(drafts, dtype=bool)[
        None
    ]
    arrived = arrived.reshape(-1, 2, block_len, head_dim)
    gathered_blocks = arrived[block_table]
    cache_keys = gathered_blocks[:, :, 0].reshape(requests, context, head_dim)
    cache_values = gathered_blocks[:, :, 1].reshape(requests, context, head_dim)
    cache_scores = jnp.einsum(
        "rqhd,rkd->rqhk", query_heads, cache_keys, preferred_element_type=jnp.float32
    )
    cache_valid = jnp.arange(context)[None, :] < cached_len[:, None]
    cache_scores = jnp.where(cache_valid[:, None, None, :], cache_scores, -jnp.inf)
    draft_scores = jnp.einsum(
        "rqhd,rpd->rqhp", query_heads, draft_keys, preferred_element_type=jnp.float32
    )
    draft_scores = jnp.where(draft_valid[:, :, None, :], draft_scores, -jnp.inf)
    row_peak = jnp.maximum(
        jnp.max(cache_scores, axis=-1, keepdims=True), jnp.max(draft_scores, axis=-1, keepdims=True)
    )
    cache_weights = jnp.exp(cache_scores - row_peak)
    draft_weights = jnp.exp(draft_scores - row_peak)
    weight_sum = jnp.sum(cache_weights, axis=-1, keepdims=True) + jnp.sum(
        draft_weights, axis=-1, keepdims=True
    )
    cache_probs = (cache_weights / weight_sum).astype(jnp.bfloat16)
    draft_probs = (draft_weights / weight_sum).astype(jnp.bfloat16)
    head_rows = jnp.einsum(
        "rqhk,rkd->rqhd", cache_probs, cache_values, preferred_element_type=jnp.float32
    )
    head_rows = head_rows + jnp.einsum(
        "rqhp,rpd->rqhd", draft_probs, draft_values, preferred_element_type=jnp.float32
    )
    heads_out = head_rows.astype(jnp.bfloat16).reshape(requests * drafts, local_heads * head_dim)
    return back(ny, nt, heads_out, w_out, w_mate)


def solution(mesh):
    placed = (
        P("groups", ("pool", "tensor")),
        P(),
        P(None, ("pool", "tensor")),
        P(("pool", "tensor"), None),
        P(("groups", "pool", "tensor"), None, None, None, None),
        P("groups", None, None),
        P("groups", None),
        P("groups"),
        P("groups", None),
    )
    return jax.shard_map(
        shards, mesh=mesh, in_specs=placed, out_specs=P("groups", None), check_vma=False
    )
```

```python
import functools

import jax
import jax.numpy as jnp
from jax import lax
from jax.experimental import pallas as pl
from jax.experimental.pallas import tpu as pltpu
from jax.sharding import PartitionSpec as P

VMEM_LIMIT = 56 * 1024 * 1024
PIECES = 2


class Place:
    def __init__(self, ny, nt):
        self.ny, self.nz, self.nt = ny, nt // ny, nt
        self.p = lax.axis_index("pool")
        self.t = lax.axis_index("tensor")
        self.y = lax.rem(self.t, ny)
        self.z = self.t // ny

    def chip(self, z, y):
        return z * self.ny + y

    def up(self, z, by):
        return lax.rem(z + by, self.nz)

    def down(self, z, by):
        return lax.rem(z + self.nz - by, self.nz)

    def rank(self, p, t):
        return p * self.nt + t

    @property
    def mate(self):
        return {"pool": 1 - self.p, "tensor": self.t}

    @property
    def across(self):
        return {"pool": self.p, "tensor": self.chip(self.z, 1 - self.y)}

    @property
    def next(self):
        return {"pool": self.p, "tensor": self.chip(self.up(self.z, 1), self.y)}

    @property
    def previous(self):
        return {"pool": self.p, "tensor": self.chip(self.down(self.z, 1), self.y)}


def remote(src, dst, send, recv, device):
    return pltpu.make_async_remote_copy(
        src_ref=src,
        dst_ref=dst,
        send_sem=send,
        recv_sem=recv,
        device_id=device,
        device_id_type=pl.DeviceIdType.MESH,
    )


def meet(devices):
    barrier = pltpu.get_barrier_semaphore()
    for device in devices:
        pl.semaphore_signal(barrier, inc=1, device_id=device, device_id_type=pl.DeviceIdType.MESH)
    pl.semaphore_wait(barrier, len(devices))


def gather_blocks(at, own, block_of, sems, use=None):
    zs, zr, ys, yr, ms, mr, ls = sems
    nz, ny = at.nz, at.ny
    part = own.shape[0] // PIECES

    def rows(ref, h):
        return ref.at[pl.ds(h * part, part), :]

    def block(p, z, y, h):
        return rows(block_of(at.rank(p, at.chip(z, y))), h)

    keep = None
    if use is None:
        keep = pltpu.make_async_copy(own, block_of(at.rank(at.p, at.t)), ls)
        keep.start()
    started = []

    def send(src, dst, send_sem, recv_sem, device):
        started.append(remote(src, dst, send_sem, recv_sem, device))
        started[-1].start()

    def ring(s, h):
        z = at.down(at.z, s)
        here = block(at.p, z, at.y, h)
        src = rows(own, h) if s == 0 else here
        if s > 0:
            remote(here, here, zs.at[s - 1, h], zr.at[s - 1, h], at.previous).wait_recv()
        if s < nz - 1:
            send(src, here, zs.at[s, h], zr.at[s, h], at.next)
        if ny == 2:
            send(src, here, ys.at[s, h], yr.at[s, h], at.across)
        send(src, here, ms.at[s, h], mr.at[s, h], at.mate)

    def from_across(s, h):
        if ny == 2:
            there = block(at.p, at.down(at.z, s), 1 - at.y, h)
            remote(there, there, ys.at[s, h], yr.at[s, h], at.across).wait_recv()
            send(there, there, ms.at[nz + s, h], mr.at[nz + s, h], at.mate)

    def step(s):
        for h in range(PIECES):
            if s < nz:
                ring(s, h)
            if s > 0:
                from_across(s - 1, h)

    def arrive(s):
        z = at.down(at.z, s)
        for y_at in range(ny):
            y = at.y if y_at == 0 else 1 - at.y
            slot = s + y_at * nz
            if use is not None and s + y_at > 0:
                use(at.rank(at.p, at.chip(z, y)))
            for h in range(PIECES):
                there = block(1 - at.p, z, y, h)
                remote(there, there, ms.at[slot, h], mr.at[slot, h], at.mate).wait_recv()
            if use is not None:
                use(at.rank(1 - at.p, at.chip(z, y)))

    def finish():
        for copy in started:
            copy.wait_send()
        if keep is not None:
            keep.wait()

    return step, arrive, finish


def gather_sems(ny, nz):
    dma = pltpu.SemaphoreType.DMA
    once, twice = dma((nz, PIECES)), dma((2 * nz, PIECES))
    return [once, once, once, once, twice, twice, dma]


def front_kernel(
    ny, nt, group_size, hidden, gain, kv, w_out, w_query, raw, blocks, w_mate,
    squares, squares_all, scales, normed, gathered, w_buf,
    zs, zr, ys, yr, ms, mr, ls, ks, kr, fs, fr, ws, wr, bs, w_sem, ss, sr,
):
    at = Place(ny, nt)
    nz = at.nz
    ranks = 2 * nt
    width = hidden.shape[1]

    def load(rank):
        start = pl.multiple_of(rank * width, width)
        return pltpu.make_async_copy(
            w_query.at[pl.ds(start, width), :], w_buf.at[rank], w_sem.at[rank]
        )

    def start_load(rank, carry):
        load(rank).start()
        return carry

    lax.fori_loop(0, ranks, start_load, 0)
    others = []
    for dt in range(nt):
        for dp in range(2):
            if dt + dp > 0:
                others.append({"pool": lax.rem(at.p + dp, 2), "tensor": lax.rem(at.t + dt, nt)})
    meet(others)
    me = at.rank(at.p, at.t)
    step, arrive, finish = gather_blocks(
        at, hidden, lambda rank: gathered.at[rank], (zs, zr, ys, yr, ms, mr, ls),
        lambda rank: use(rank),
    )
    step(0)

    wide = hidden[...].astype(jnp.float32)
    squares[...] = lax.dot_general(
        jnp.ones((8, width), jnp.float32), wide * wide, (((1,), (1,)), ((), ())),
        precision=lax.Precision.HIGHEST, preferred_element_type=jnp.float32,
    )
    square_copies = [
        remote(squares, squares_all.at[i], ss.at[i], sr.at[i], device)
        for i, device in enumerate(others)
    ]
    for copy in square_copies:
        copy.start()

    def head_of(p, t):
        return at.rank(p, t) // group_size

    keep = pltpu.make_async_copy(kv.at[:, head_of(at.p, at.t)], blocks.at[me], bs)
    keep.start()
    half = w_mate.shape[1]
    swap = remote(
        w_out.at[:, pl.ds(pl.multiple_of((1 - at.p) * half, half), half)],
        w_mate, ws, wr, at.mate,
    )
    sends = []
    for dz in range(nz):
        for dp in range(2):
            if dz + dp > 0:
                device = {
                    "pool": lax.rem(at.p + dp, 2),
                    "tensor": at.chip(at.up(at.z, dz), at.y),
                }
                slot = dz * 2 + dp
                head = head_of(device["pool"], device["tensor"])
                sends.append(remote(kv.at[:, head], blocks.at[me], ks.at[slot], kr.at[slot], device))
                sends[-1].start()

    def use(rank):
        load(rank).wait()
        start = pl.multiple_of(rank * width, width)
        for c in range(width // 128):
            lanes = slice(c * 128, (c + 1) * 128)
            features = pl.ds(pl.multiple_of(start + c * 128, 128), 128)
            normed[:, lanes] = (
                gathered[rank, :, lanes].astype(jnp.float32) * scales[...] * gain[:, features]
            ).astype(normed.dtype)
        raw[...] += jnp.dot(normed[...], w_buf[rank], preferred_element_type=jnp.float32)

    def sum_squares():
        total = squares[...]
        for i, copy in enumerate(square_copies):
            copy.wait_recv()
            total = total + squares_all[i]
        scale = lax.rsqrt(total * (1.0 / (width * ranks)) + 1e-05)
        scales[...] = jnp.transpose(jnp.concatenate([scale] * 16, axis=0))

    def block_from(dz, dp):
        return at.rank(lax.rem(at.p + dp, 2), at.chip(at.down(at.z, dz), at.y))

    def forward(dz):
        for dp in range(2):
            slot = dz * 2 + dp
            here = blocks.at[block_from(dz, dp)]
            src = here
            if slot == 0:
                src = kv.at[:, head_of(at.p, at.t)]
            else:
                remote(here, here, ks.at[slot], kr.at[slot], at.mate).wait_recv()
            if ny == 2:
                sends.append(remote(src, here, fs.at[slot], fr.at[slot], at.across))
                sends[-1].start()

    forward(0)
    swap.start()
    gathered[me] = hidden[...]
    raw[...] = jnp.zeros_like(raw)
    sum_squares()
    use(me)
    for s in range(1, nz + 1):
        step(s)
        if s < nz:
            forward(s)
        arrive(s - 1)
    finish()
    if ny == 2:
        for dz in range(nz):
            for dp in range(2):
                slot = dz * 2 + dp
                source = at.rank(
                    lax.rem(at.p + dp, 2), at.chip(at.down(at.z, dz), 1 - at.y)
                )
                there = blocks.at[source]
                remote(there, there, fs.at[slot], fr.at[slot], at.across).wait_recv()
    for copy in sends + square_copies:
        copy.wait_send()
    swap.wait()
    keep.wait()


def front(ny, nt, group_size, hidden, gain, kv_pool, w_out, w_query):
    rows, width = hidden.shape
    columns = w_query.shape[1]
    nz = nt // ny
    ranks = 2 * nt
    dma = pltpu.SemaphoreType.DMA
    blocks = (ranks, kv_pool.shape[0]) + kv_pool.shape[2:]
    return pl.pallas_call(
        functools.partial(front_kernel, ny, nt, group_size),
        out_shape=(
            jax.ShapeDtypeStruct((rows, columns), jnp.float32),
            jax.ShapeDtypeStruct(blocks, kv_pool.dtype),
            jax.ShapeDtypeStruct((w_out.shape[0], w_out.shape[1] // 2), w_out.dtype),
        ),
        in_specs=[pl.BlockSpec(memory_space=pltpu.VMEM)] * 2
        + [pl.BlockSpec(memory_space=pl.ANY)] * 3,
        out_specs=(
            pl.BlockSpec(memory_space=pltpu.VMEM),
            pl.BlockSpec(memory_space=pl.ANY),
            pl.BlockSpec(memory_space=pl.ANY),
        ),
        scratch_shapes=[
            pltpu.VMEM((8, rows), jnp.float32),
            pltpu.VMEM((ranks - 1, 8, rows), jnp.float32),
            pltpu.VMEM((rows, 128), jnp.float32),
            pltpu.VMEM((rows, width), hidden.dtype),
            pltpu.VMEM((ranks, rows, width), hidden.dtype),
            pltpu.VMEM((ranks, width, columns), w_query.dtype),
        ]
        + gather_sems(ny, nz)
        + [dma((2 * nz,)), dma((2 * nz,)), dma((2 * nz,)), dma((2 * nz,)), dma, dma, dma]
        + [dma((ranks,)), dma((ranks - 1,)), dma((ranks - 1,))],
        compiler_params=pltpu.CompilerParams(
            collective_id=0, has_side_effects=True, vmem_limit_bytes=VMEM_LIMIT
        ),
        name="front",
    )(hidden, gain, kv_pool, w_out, w_query)


def code(value, codes, scales):
    peak = jnp.maximum(jnp.max(jnp.abs(value), axis=0, keepdims=True), 1e-30)
    codes[...] = jnp.round(value * (32767.0 / peak)).astype(jnp.int32).astype(jnp.int16)
    scales[...] = jnp.broadcast_to(peak * (1.0 / 32767.0), scales.shape)


def decode(codes, scales):
    return codes[...].astype(jnp.int32).astype(jnp.float32) * scales[0:1, :]


def back_kernel(
    ny, nt, heads, w_own, w_mate, out,
    heads_mate, w_buf, y_send, y_recv, z_send, z_recv,
    y_send_scale, y_recv_scale, z_send_scale, z_recv_scale, final,
    hs, hr, w_sem, ps, pr, qs, qr, pss, psr, qss, qsr, zs, zr, ys, yr, ms, mr, ls,
):
    at = Place(ny, nt)
    nz = at.nz
    width = final.shape[1]
    half = w_mate.shape[1]

    def load(which, t):
        if which == 0:
            start = pl.multiple_of(at.p * half + t * width, width)
            src = w_own.at[:, pl.ds(start, width)]
        else:
            src = w_mate.at[:, pl.ds(pl.multiple_of(t * width, width), width)]
        return pltpu.make_async_copy(src, w_buf.at[which, t], w_sem.at[which, t])

    def chunk(s):
        return at.down(at.z, s + 1)

    def chip_of(s, y):
        return at.chip(lax.rem(at.z + 2 * nz - 1 - s, nz), y)

    def start_loads(y):
        def body(s, carry):
            t = chip_of(s, y)
            load(0, t).start()
            load(1, t).start()
            return carry

        lax.fori_loop(0, nz, body, 0)

    if ny == 2:
        start_loads(1 - at.y)
    start_loads(at.y)
    neighbours = [at.mate, at.next, at.previous] + ([at.across] if ny == 2 else [])
    meet(neighbours)
    trade = remote(heads, heads_mate, hs, hr, at.mate)
    trade.start()
    trade.wait()

    def term(t):
        load(0, t).wait()
        load(1, t).wait()
        return jnp.dot(heads[...], w_buf[0, t], preferred_element_type=jnp.float32) + jnp.dot(
            heads_mate[...], w_buf[1, t], preferred_element_type=jnp.float32
        )

    def across_copies(s):
        return [
            remote(y_send.at[s], y_recv.at[s], ps.at[s], pr.at[s], at.across),
            remote(y_send_scale.at[s], y_recv_scale.at[s], pss.at[s], psr.at[s], at.across),
        ]

    def ring_copies(s):
        return [
            remote(z_send.at[s], z_recv.at[s], qs.at[s], qr.at[s], at.next),
            remote(z_send_scale.at[s], z_recv_scale.at[s], qss.at[s], qsr.at[s], at.next),
        ]

    if ny == 2:

        def send_across(s, carry):
            code(term(chip_of(s, 1 - at.y)), y_send.at[s], y_send_scale.at[s])
            for copy in across_copies(s):
                copy.start()
            return carry

        lax.fori_loop(0, nz, send_across, 0)

    def total(s):
        value = term(chip_of(s, at.y))
        if ny == 2:
            for copy in across_copies(s):
                copy.wait_recv()
            value = value + decode(y_recv.at[s], y_recv_scale.at[s])
        return value

    def ring_received(s):
        for copy in ring_copies(s):
            copy.wait_recv()
        return decode(z_recv.at[s], z_recv_scale.at[s])

    def ring_send(s, value):
        code(value, z_send.at[s], z_send_scale.at[s])
        for copy in ring_copies(s):
            copy.start()

    ring_send(0, total(0))

    def ring_step(s, carry):
        value = total(s)
        ring_send(s, value + ring_received(s - 1))
        return carry

    lax.fori_loop(1, nz - 1, ring_step, 0)
    value = total(nz - 1)
    final[...] = (value + ring_received(nz - 2)).astype(final.dtype)

    def block_of(rank):
        return out.at[:, pl.ds(pl.multiple_of(rank * width, width), width)]

    step, arrive, finish = gather_blocks(at, final, block_of, (zs, zr, ys, yr, ms, mr, ls))
    for s in range(nz + 1):
        step(s)
    for s in range(nz):
        arrive(s)
    finish()

    def sent(s, carry):
        if ny == 2:
            for copy in across_copies(s):
                copy.wait_send()
        return carry

    lax.fori_loop(0, nz, sent, 0)

    def ring_sent(s, carry):
        for copy in ring_copies(s):
            copy.wait_send()
        return carry

    lax.fori_loop(0, nz - 1, ring_sent, 0)


def back(ny, nt, heads, w_out, w_mate):
    rows, depth = heads.shape
    columns = w_out.shape[1]
    nz = nt // ny
    width = columns // (2 * nt)
    dma = pltpu.SemaphoreType.DMA
    f32 = jnp.float32
    return pl.pallas_call(
        functools.partial(back_kernel, ny, nt),
        out_shape=jax.ShapeDtypeStruct((rows, columns), jnp.bfloat16),
        in_specs=[
            pl.BlockSpec(memory_space=pltpu.VMEM),
            pl.BlockSpec(memory_space=pl.ANY),
            pl.BlockSpec(memory_space=pl.ANY),
        ],
        out_specs=pl.BlockSpec(memory_space=pl.ANY),
        scratch_shapes=[
            pltpu.VMEM((rows, depth), heads.dtype),
            pltpu.VMEM((2, nt, depth, width), w_out.dtype),
            pltpu.VMEM((nz, rows, width), jnp.int16),
            pltpu.VMEM((nz, rows, width), jnp.int16),
            pltpu.VMEM((nz - 1, rows, width), jnp.int16),
            pltpu.VMEM((nz - 1, rows, width), jnp.int16),
            pltpu.VMEM((nz, 8, width), f32),
            pltpu.VMEM((nz, 8, width), f32),
            pltpu.VMEM((nz - 1, 8, width), f32),
            pltpu.VMEM((nz - 1, 8, width), f32),
            pltpu.VMEM((rows, width), jnp.bfloat16),
            dma,
            dma,
            dma((2, nt)),
            dma((nz,)),
            dma((nz,)),
            dma((nz,)),
            dma((nz,)),
            dma((nz,)),
            dma((nz,)),
            dma((nz,)),
            dma((nz,)),
        ]
        + gather_sems(ny, nz),
        compiler_params=pltpu.CompilerParams(
            collective_id=1, has_side_effects=True, vmem_limit_bytes=VMEM_LIMIT
        ),
        name="back",
    )(heads, w_out, w_mate)


def attention_kernel(
    table, lengths, raw, cosine, sine, draft_k, draft_v, draft_bias, blocks, out, keys, values, sems
):
    request = pl.program_id(0)
    requests, context, head_dim = keys.shape
    block_len = blocks.shape[2]
    listed = context // block_len

    def copies(r, j):
        here = pl.ds(pl.multiple_of(j * block_len, block_len), block_len)
        block = table[r, j]
        return [
            pltpu.make_async_copy(blocks.at[block, 0], keys.at[r, here, :], sems.at[0, r, j]),
            pltpu.make_async_copy(blocks.at[block, 1], values.at[r, here, :], sems.at[1, r, j]),
        ]

    @pl.when(request == 0)
    def _():
        def start(i, carry):
            for copy in copies(i // listed, lax.rem(i, listed)):
                copy.start()
            return carry

        lax.fori_loop(0, requests * listed, start, 0)

    def arrived(j, carry):
        for copy in copies(request, j):
            copy.wait()
        return carry

    lax.fori_loop(0, listed, arrived, 0)
    both = (((1,), (1,)), ((), ()))
    f32 = jnp.float32
    valid = lax.broadcasted_iota(jnp.int32, (1, context), 1) < lengths[request]
    for h in range(raw.shape[1] // head_dim):
        lanes = slice(h * head_dim, (h + 1) * head_dim)
        query = raw[:, lanes]
        swapped = jnp.concatenate(
            [query[:, head_dim // 2 :], query[:, : head_dim // 2]], axis=1
        )
        query = query * cosine[...] + swapped * sine[...]
        query = (query * head_dim ** (-0.5)).astype(jnp.bfloat16)
        cache = lax.dot_general(query, keys[request], both, preferred_element_type=f32)
        cache = jnp.where(valid, cache, -jnp.inf)
        draft = lax.dot_general(query, draft_k[...], both, preferred_element_type=f32)
        draft = draft + draft_bias[0]
        peak = jnp.maximum(
            jnp.max(cache, axis=-1, keepdims=True), jnp.max(draft, axis=-1, keepdims=True)
        )
        cache = jnp.exp(cache - peak)
        draft = jnp.exp(draft - peak)
        share = 1.0 / (
            jnp.sum(cache, axis=-1, keepdims=True) + jnp.sum(draft, axis=-1, keepdims=True)
        )
        cache = (cache * share).astype(jnp.bfloat16)
        draft = (draft * share).astype(jnp.bfloat16)
        rows = jnp.dot(cache, values[request], preferred_element_type=f32)
        rows = rows + jnp.dot(draft, draft_v[...], preferred_element_type=f32)
        out[:, lanes] = rows.astype(out.dtype)


def attention(raw, cosine, sine, draft_k, draft_v, draft_bias, blocks, table, lengths):
    rows, columns = raw.shape
    requests, listed = table.shape
    drafts = rows // requests
    block_len, head_dim = blocks.shape[2:]
    context = listed * block_len

    def by_rows(width):
        return pl.BlockSpec((drafts, width), lambda r, *_: (r, 0))

    return pl.pallas_call(
        attention_kernel,
        out_shape=jax.ShapeDtypeStruct((rows, columns), jnp.bfloat16),
        grid_spec=pltpu.PrefetchScalarGridSpec(
            num_scalar_prefetch=2,
            grid=(requests,),
            in_specs=[
                by_rows(columns),
                by_rows(head_dim),
                by_rows(head_dim),
                by_rows(head_dim),
                by_rows(head_dim),
                pl.BlockSpec((1, drafts, drafts), lambda r, *_: (r, 0, 0)),
                pl.BlockSpec(memory_space=pl.ANY),
            ],
            out_specs=by_rows(columns),
            scratch_shapes=[
                pltpu.VMEM((requests, context, head_dim), blocks.dtype),
                pltpu.VMEM((requests, context, head_dim), blocks.dtype),
                pltpu.SemaphoreType.DMA((2, requests, listed)),
            ],
        ),
        compiler_params=pltpu.CompilerParams(
            dimension_semantics=("arbitrary",), vmem_limit_bytes=VMEM_LIMIT
        ),
        name="mid",
    )(table, lengths, raw, cosine, sine, draft_k, draft_v, draft_bias, blocks)


def shards(
    hidden, norm_gain, w_query, w_out, kv_pool, draft_kv, block_table, cached_len, draft_pos
):
    nt = lax.axis_size("tensor")
    ny = 2 if nt == 8 else 1
    devices = lax.axis_size(("pool", "tensor"))
    my_rank = lax.axis_index(("pool", "tensor"))
    kv_heads = kv_pool.shape[1]
    block_len = kv_pool.shape[3]
    head_dim = kv_pool.shape[4]
    drafts = draft_pos.shape[1]
    group_size = devices // kv_heads
    own_head = my_rank // group_size
    gain = norm_gain.reshape(1, -1)
    raw_queries, arrived, w_mate = front(
        ny, nt, group_size, hidden, gain, kv_pool, w_out, w_query
    )
    positions = (cached_len[:, None] + draft_pos).reshape(-1)
    half_dim = head_dim // 2
    frequency = 500000.0 ** (-(jnp.arange(half_dim, dtype=jnp.float32) * 2.0) / head_dim)
    angles = positions.astype(jnp.float32)[:, None] * frequency[None, :]
    cosine, sine = jnp.cos(angles), jnp.sin(angles)
    cosine = jnp.concatenate([cosine, cosine], axis=-1)
    sine = jnp.concatenate([-sine, sine], axis=-1)
    own_draft = lax.dynamic_slice_in_dim(draft_kv, own_head * head_dim, head_dim, axis=2)
    draft_valid = (draft_pos[:, None, :] < draft_pos[:, :, None]) | jnp.eye(drafts, dtype=bool)[
        None
    ]
    draft_bias = jnp.where(draft_valid, 0.0, -jnp.inf).astype(jnp.float32)
    blocks = arrived.reshape(-1, 2, block_len, head_dim)
    heads_out = attention(
        raw_queries, cosine, sine, own_draft[:, 0], own_draft[:, 1], draft_bias,
        blocks, block_table, cached_len,
    )
    return back(ny, nt, heads_out, w_out, w_mate)


def solution(mesh):
    placed = (
        P("groups", ("pool", "tensor")),
        P(),
        P(None, ("pool", "tensor")),
        P(("pool", "tensor"), None),
        P(("groups", "pool", "tensor"), None, None, None, None),
        P("groups", None, None),
        P("groups", None),
        P("groups"),
        P("groups", None),
    )
    return jax.shard_map(
        shards, mesh=mesh, in_specs=placed, out_specs=P("groups", None), check_vma=False
    )
```

```python
import functools

import jax
import jax.numpy as jnp
import numpy as np
from jax import lax
from jax.experimental import pallas as pl
from jax.experimental.pallas import tpu as pltpu
from jax.sharding import PartitionSpec as P

VMEM_LIMIT = 56 * 1024 * 1024
PIECES = 2


class Place:
    def __init__(self, ny, nt):
        self.ny, self.nz, self.nt = ny, nt // ny, nt
        self.p = lax.axis_index("pool")
        self.t = lax.axis_index("tensor")
        self.y = lax.rem(self.t, ny)
        self.z = self.t // ny

    def chip(self, z, y):
        return z * self.ny + y

    def up(self, z, by):
        return lax.rem(z + by, self.nz)

    def down(self, z, by):
        return lax.rem(z + self.nz - by, self.nz)

    def rank(self, p, t):
        return p * self.nt + t

    @property
    def mate(self):
        return {"pool": 1 - self.p, "tensor": self.t}

    @property
    def across(self):
        return {"pool": self.p, "tensor": self.chip(self.z, 1 - self.y)}

    @property
    def next(self):
        return {"pool": self.p, "tensor": self.chip(self.up(self.z, 1), self.y)}

    @property
    def previous(self):
        return {"pool": self.p, "tensor": self.chip(self.down(self.z, 1), self.y)}


def remote(src, dst, send, recv, device):
    return pltpu.make_async_remote_copy(
        src_ref=src,
        dst_ref=dst,
        send_sem=send,
        recv_sem=recv,
        device_id=device,
        device_id_type=pl.DeviceIdType.MESH,
    )


def meet(devices):
    barrier = pltpu.get_barrier_semaphore()
    for device in devices:
        pl.semaphore_signal(barrier, inc=1, device_id=device, device_id_type=pl.DeviceIdType.MESH)
    pl.semaphore_wait(barrier, len(devices))


def gather_blocks(at, own, block_of, sems, use=None, keep_last=False):
    zs, zr, ys, yr, ms, mr, ls = sems
    nz, ny = at.nz, at.ny
    part = own.shape[0] // PIECES

    def rows(ref, h):
        return ref.at[pl.ds(h * part, part), :]

    def block(p, z, y, h):
        return rows(block_of(at.rank(p, at.chip(z, y))), h)

    if keep_last:
        keep = pltpu.make_async_copy(own, block_of(at.rank(at.p, at.t)), ls)
    started = []

    def send(src, dst, send_sem, recv_sem, device):
        started.append(remote(src, dst, send_sem, recv_sem, device))
        started[-1].start()

    def ring(s, h):
        z = at.down(at.z, s)
        here = block(at.p, z, at.y, h)
        src = rows(own, h) if s == 0 else here
        if s > 0:
            remote(here, here, zs.at[s - 1, h], zr.at[s - 1, h], at.previous).wait_recv()
        if s < nz - 1:
            send(src, here, zs.at[s, h], zr.at[s, h], at.next)
        if ny == 2:
            send(src, here, ys.at[s, h], yr.at[s, h], at.across)
        send(src, here, ms.at[s, h], mr.at[s, h], at.mate)

    def from_across(s, h):
        if ny == 2:
            there = block(at.p, at.down(at.z, s), 1 - at.y, h)
            remote(there, there, ys.at[s, h], yr.at[s, h], at.across).wait_recv()
            send(there, there, ms.at[nz + s, h], mr.at[nz + s, h], at.mate)

    def step(s, pieces=range(PIECES)):
        for h in pieces:
            if s < nz:
                ring(s, h)
            if s > 0:
                from_across(s - 1, h)
            if keep_last and s == 0 and h == PIECES - 1:
                keep.start()

    def arrive(s):
        z = at.down(at.z, s)
        for y_at in range(ny):
            y = at.y if y_at == 0 else 1 - at.y
            slot = s + y_at * nz
            if use is not None and s + y_at > 0:
                use(at.rank(at.p, at.chip(z, y)))
            for h in range(PIECES):
                there = block(1 - at.p, z, y, h)
                remote(there, there, ms.at[slot, h], mr.at[slot, h], at.mate).wait_recv()
            if use is not None:
                use(at.rank(1 - at.p, at.chip(z, y)))

    def finish():
        for copy in started:
            copy.wait_send()
        if keep_last:
            keep.wait()

    return step, arrive, finish


def gather_sems(ny, nz):
    dma = pltpu.SemaphoreType.DMA
    once, twice = dma((nz, PIECES)), dma((2 * nz, PIECES))
    return [once, once, once, once, twice, twice, dma]


def front_kernel(
    ny, nt, group_size, hidden, gain, kv, w_out, w_query, raw, blocks, w_mate,
    squares, squares_all, scales, normed, gathered, w_buf,
    zs, zr, ys, yr, ms, mr, ls, ks, kr, fs, fr, ws, wr, bs, w_sem, ss, sr,
):
    at = Place(ny, nt)
    nz = at.nz
    ranks = 2 * nt
    width = hidden.shape[1]

    def load(rank):
        start = pl.multiple_of(rank * width, width)
        return pltpu.make_async_copy(
            w_query.at[pl.ds(start, width), :], w_buf.at[rank], w_sem.at[rank]
        )

    def start_load(rank, carry):
        load(rank).start()
        return carry

    lax.fori_loop(0, ranks, start_load, 0)
    others = []
    for dt in range(nt):
        for dp in range(2):
            if dt + dp > 0:
                others.append({"pool": lax.rem(at.p + dp, 2), "tensor": lax.rem(at.t + dt, nt)})
    meet(others)
    me = at.rank(at.p, at.t)
    step, arrive, finish = gather_blocks(
        at, hidden, lambda rank: gathered.at[rank], (zs, zr, ys, yr, ms, mr, ls),
        lambda rank: use(rank),
    )
    step(0)

    wide = hidden[...].astype(jnp.float32)
    squares[...] = lax.dot_general(
        jnp.ones((8, width), jnp.float32), wide * wide, (((1,), (1,)), ((), ())),
        precision=lax.Precision.HIGHEST, preferred_element_type=jnp.float32,
    )
    square_copies = [
        remote(squares, squares_all.at[i], ss.at[i], sr.at[i], device)
        for i, device in enumerate(others)
    ]
    for copy in square_copies:
        copy.start()

    def head_of(p, t):
        return at.rank(p, t) // group_size

    keep = pltpu.make_async_copy(kv.at[:, head_of(at.p, at.t)], blocks.at[me], bs)
    keep.start()
    half = w_mate.shape[1]
    swap = remote(
        w_out.at[:, pl.ds(pl.multiple_of((1 - at.p) * half, half), half)],
        w_mate, ws, wr, at.mate,
    )
    sends = []

    def send_blocks(dz):
        for dp in range(2):
            if dz + dp > 0:
                device = {
                    "pool": lax.rem(at.p + dp, 2),
                    "tensor": at.chip(at.up(at.z, dz), at.y),
                }
                slot = dz * 2 + dp
                head = head_of(device["pool"], device["tensor"])
                sends.append(remote(kv.at[:, head], blocks.at[me], ks.at[slot], kr.at[slot], device))
                sends[-1].start()

    send_blocks(0)

    def use(rank):
        load(rank).wait()
        start = pl.multiple_of(rank * width, width)
        for c in range(width // 128):
            lanes = slice(c * 128, (c + 1) * 128)
            features = pl.ds(pl.multiple_of(start + c * 128, 128), 128)
            normed[:, lanes] = (
                gathered[rank, :, lanes].astype(jnp.float32) * scales[...] * gain[:, features]
            ).astype(normed.dtype)
        raw[...] += jnp.dot(normed[...], w_buf[rank], preferred_element_type=jnp.float32)

    def sum_squares():
        total = squares[...]
        for i, copy in enumerate(square_copies):
            copy.wait_recv()
            total = total + squares_all[i]
        scale = lax.rsqrt(total * (1.0 / (width * ranks)) + 1e-05)
        scales[...] = jnp.transpose(jnp.concatenate([scale] * 16, axis=0))

    def block_from(dz, dp):
        return at.rank(lax.rem(at.p + dp, 2), at.chip(at.down(at.z, dz), at.y))

    def forward(dz):
        for dp in range(2):
            slot = dz * 2 + dp
            here = blocks.at[block_from(dz, dp)]
            src = here
            if slot == 0:
                src = kv.at[:, head_of(at.p, at.t)]
            else:
                remote(here, here, ks.at[slot], kr.at[slot], at.mate).wait_recv()
            if ny == 2:
                sends.append(remote(src, here, fs.at[slot], fr.at[slot], at.across))
                sends[-1].start()

    forward(0)
    swap.start()
    gathered[me] = hidden[...]
    raw[...] = jnp.zeros_like(raw)
    sum_squares()
    use(me)
    for s in range(1, nz + 1):
        step(s)
        if s < nz:
            send_blocks(s)
        if s > 1:
            forward(s - 1)
        arrive(s - 1)
    finish()
    if ny == 2:
        for dz in range(nz):
            for dp in range(2):
                slot = dz * 2 + dp
                source = at.rank(
                    lax.rem(at.p + dp, 2), at.chip(at.down(at.z, dz), 1 - at.y)
                )
                there = blocks.at[source]
                remote(there, there, fs.at[slot], fr.at[slot], at.across).wait_recv()
    for copy in sends + square_copies:
        copy.wait_send()
    swap.wait()
    keep.wait()


def front(ny, nt, group_size, hidden, gain, kv_pool, w_out, w_query):
    rows, width = hidden.shape
    columns = w_query.shape[1]
    nz = nt // ny
    ranks = 2 * nt
    dma = pltpu.SemaphoreType.DMA
    blocks = (ranks, kv_pool.shape[0]) + kv_pool.shape[2:]
    return pl.pallas_call(
        functools.partial(front_kernel, ny, nt, group_size),
        out_shape=(
            jax.ShapeDtypeStruct((rows, columns), jnp.float32),
            jax.ShapeDtypeStruct(blocks, kv_pool.dtype),
            jax.ShapeDtypeStruct((w_out.shape[0], w_out.shape[1] // 2), w_out.dtype),
        ),
        in_specs=[pl.BlockSpec(memory_space=pltpu.VMEM)] * 2
        + [pl.BlockSpec(memory_space=pl.ANY)] * 3,
        out_specs=(
            pl.BlockSpec(memory_space=pltpu.VMEM),
            pl.BlockSpec(memory_space=pl.ANY),
            pl.BlockSpec(memory_space=pl.ANY),
        ),
        scratch_shapes=[
            pltpu.VMEM((8, rows), jnp.float32),
            pltpu.VMEM((ranks - 1, 8, rows), jnp.float32),
            pltpu.VMEM((rows, 128), jnp.float32),
            pltpu.VMEM((rows, width), hidden.dtype),
            pltpu.VMEM((ranks, rows, width), hidden.dtype),
            pltpu.VMEM((ranks, width, columns), w_query.dtype),
        ]
        + gather_sems(ny, nz)
        + [dma((2 * nz,)), dma((2 * nz,)), dma((2 * nz,)), dma((2 * nz,)), dma, dma, dma]
        + [dma((ranks,)), dma((ranks - 1,)), dma((ranks - 1,))],
        compiler_params=pltpu.CompilerParams(
            collective_id=0, has_side_effects=True, vmem_limit_bytes=VMEM_LIMIT
        ),
        name="front",
    )(hidden, gain, kv_pool, w_out, w_query)


def code(value, codes, scales):
    peak = jnp.maximum(jnp.max(jnp.abs(value), axis=0, keepdims=True), 1e-30)
    codes[...] = jnp.round(value * (32767.0 / peak)).astype(jnp.int32).astype(jnp.int16)
    scales[...] = jnp.broadcast_to(peak * (1.0 / 32767.0), scales.shape)


def decode(codes, scales):
    return codes[...].astype(jnp.int32).astype(jnp.float32) * scales[0:1, :]


def back_kernel(
    ny, nt, heads, w_own, w_mate, out,
    heads_mate, w_buf, y_send, y_recv, z_send, z_recv,
    y_send_scale, y_recv_scale, z_send_scale, z_recv_scale, final,
    hs, hr, w_sem, ps, pr, qs, qr, pss, psr, qss, qsr, zs, zr, ys, yr, ms, mr, ls,
):
    at = Place(ny, nt)
    nz = at.nz
    width = final.shape[1]
    half = w_mate.shape[1]

    def load(which, t):
        if which == 0:
            start = pl.multiple_of(at.p * half + t * width, width)
            src = w_own.at[:, pl.ds(start, width)]
        else:
            src = w_mate.at[:, pl.ds(pl.multiple_of(t * width, width), width)]
        return pltpu.make_async_copy(src, w_buf.at[which, t], w_sem.at[which, t])

    part = heads.shape[0] // PIECES

    def chip_of(s, y):
        return at.chip(lax.rem(at.z + 2 * nz - 1 - s, nz), y)

    def start_loads(y):
        def body(s, carry):
            t = chip_of(s, y)
            load(0, t).start()
            load(1, t).start()
            return carry

        lax.fori_loop(0, nz, body, 0)

    if ny == 2:
        start_loads(1 - at.y)
    start_loads(at.y)
    neighbours = [at.mate, at.next, at.previous] + ([at.across] if ny == 2 else [])
    meet(neighbours)
    trade = remote(heads, heads_mate, hs, hr, at.mate)
    trade.start()
    trade.wait()

    def rows_of(i):
        return pl.ds(pl.multiple_of(lax.rem(i, PIECES) * part, part), part)

    def wait_loads(y):
        def body(s, carry):
            t = chip_of(s, y)
            load(0, t).wait()
            load(1, t).wait()
            return carry

        lax.fori_loop(0, nz, body, 0)

    def term(i, y):
        t = chip_of(i // PIECES, y)
        return jnp.dot(
            heads[rows_of(i), :], w_buf[0, t], preferred_element_type=jnp.float32
        ) + jnp.dot(heads_mate[rows_of(i), :], w_buf[1, t], preferred_element_type=jnp.float32)

    def across_copies(i):
        return [
            remote(y_send.at[i], y_recv.at[i], ps.at[i], pr.at[i], at.across),
            remote(y_send_scale.at[i], y_recv_scale.at[i], pss.at[i], psr.at[i], at.across),
        ]

    def ring_copies(i):
        return [
            remote(z_send.at[i], z_recv.at[i], qs.at[i], qr.at[i], at.next),
            remote(z_send_scale.at[i], z_recv_scale.at[i], qss.at[i], qsr.at[i], at.next),
        ]

    if ny == 2:
        wait_loads(1 - at.y)

        def send_across(i, carry):
            code(term(i, 1 - at.y), y_send.at[i], y_send_scale.at[i])
            for copy in across_copies(i):
                copy.start()
            return carry

        lax.fori_loop(0, nz * PIECES, send_across, 0)
    wait_loads(at.y)

    def total(i):
        value = term(i, at.y)
        if ny == 2:
            for copy in across_copies(i):
                copy.wait_recv()
            value = value + decode(y_recv.at[i], y_recv_scale.at[i])
        return value

    def ring_received(i):
        for copy in ring_copies(i):
            copy.wait_recv()
        return decode(z_recv.at[i], z_recv_scale.at[i])

    def ring_send(i, value):
        code(value, z_send.at[i], z_send_scale.at[i])
        for copy in ring_copies(i):
            copy.start()

    def ring_first(i, carry):
        ring_send(i, total(i))
        return carry

    lax.fori_loop(0, PIECES, ring_first, 0)

    def ring_step(i, carry):
        value = total(i)
        ring_send(i, value + ring_received(i - PIECES))
        return carry

    lax.fori_loop(PIECES, (nz - 1) * PIECES, ring_step, 0)

    def block_of(rank):
        return out.at[:, pl.ds(pl.multiple_of(rank * width, width), width)]

    step, arrive, finish = gather_blocks(
        at, final, block_of, (zs, zr, ys, yr, ms, mr, ls), keep_last=True
    )
    for h in range(PIECES):
        i = (nz - 1) * PIECES + h
        value = total(i)
        final[h * part : (h + 1) * part, :] = (value + ring_received(i - PIECES)).astype(
            final.dtype
        )
        step(0, (h,))
    for s in range(1, nz + 1):
        step(s)
    for s in range(nz):
        arrive(s)
    finish()

    def sent(i, carry):
        if ny == 2:
            for copy in across_copies(i):
                copy.wait_send()
        return carry

    lax.fori_loop(0, nz * PIECES, sent, 0)

    def ring_sent(s, carry):
        for copy in ring_copies(s):
            copy.wait_send()
        return carry

    lax.fori_loop(0, (nz - 1) * PIECES, ring_sent, 0)


def back(ny, nt, heads, w_out, w_mate):
    rows, depth = heads.shape
    columns = w_out.shape[1]
    nz = nt // ny
    width = columns // (2 * nt)
    dma = pltpu.SemaphoreType.DMA
    f32 = jnp.float32
    return pl.pallas_call(
        functools.partial(back_kernel, ny, nt),
        out_shape=jax.ShapeDtypeStruct((rows, columns), jnp.bfloat16),
        in_specs=[
            pl.BlockSpec(memory_space=pltpu.VMEM),
            pl.BlockSpec(memory_space=pl.ANY),
            pl.BlockSpec(memory_space=pl.ANY),
        ],
        out_specs=pl.BlockSpec(memory_space=pl.ANY),
        scratch_shapes=[
            pltpu.VMEM((rows, depth), heads.dtype),
            pltpu.VMEM((2, nt, depth, width), w_out.dtype),
            pltpu.VMEM((nz * PIECES, rows // PIECES, width), jnp.int16),
            pltpu.VMEM((nz * PIECES, rows // PIECES, width), jnp.int16),
            pltpu.VMEM(((nz - 1) * PIECES, rows // PIECES, width), jnp.int16),
            pltpu.VMEM(((nz - 1) * PIECES, rows // PIECES, width), jnp.int16),
            pltpu.VMEM((nz * PIECES, 8, width), f32),
            pltpu.VMEM((nz * PIECES, 8, width), f32),
            pltpu.VMEM(((nz - 1) * PIECES, 8, width), f32),
            pltpu.VMEM(((nz - 1) * PIECES, 8, width), f32),
            pltpu.VMEM((rows, width), jnp.bfloat16),
            dma,
            dma,
            dma((2, nt)),
            dma((nz * PIECES,)),
            dma((nz * PIECES,)),
            dma((nz * PIECES,)),
            dma((nz * PIECES,)),
            dma((nz * PIECES,)),
            dma((nz * PIECES,)),
            dma((nz * PIECES,)),
            dma((nz * PIECES,)),
        ]
        + gather_sems(ny, nz),
        compiler_params=pltpu.CompilerParams(
            collective_id=1, has_side_effects=True, vmem_limit_bytes=VMEM_LIMIT
        ),
        name="back",
    )(heads, w_out, w_mate)


def attention_kernel(
    table, lengths, head, raw, depth_down, depth_along, frequency, draft_kv, blocks, out, keys, values, sems
):
    request = pl.program_id(0)
    requests, context, head_dim = keys.shape
    block_len = blocks.shape[2]
    listed = context // block_len

    def copies(r, j):
        here = pl.ds(pl.multiple_of(j * block_len, block_len), block_len)
        block = table[r, j]
        return [
            pltpu.make_async_copy(blocks.at[block, 0], keys.at[r, here, :], sems.at[0, r, j]),
            pltpu.make_async_copy(blocks.at[block, 1], values.at[r, here, :], sems.at[1, r, j]),
        ]

    @pl.when(request == 0)
    def _():
        def start(i, carry):
            for copy in copies(i // listed, lax.rem(i, listed)):
                copy.start()
            return carry

        lax.fori_loop(0, requests * listed, start, 0)

    def arrived(j, carry):
        for copy in copies(request, j):
            copy.wait()
        return carry

    lax.fori_loop(0, listed, arrived, 0)
    both = (((1,), (1,)), ((), ()))
    f32 = jnp.float32
    valid = lax.broadcasted_iota(jnp.int32, (1, context), 1) < lengths[request]
    drafts = raw.shape[0]
    angles = (lengths[request] + depth_down[...]).astype(f32) * frequency[...]
    cosine = jnp.cos(angles)
    sine = jnp.sin(angles)
    sine = jnp.where(
        lax.broadcasted_iota(jnp.int32, (1, head_dim), 1) < head_dim // 2, -sine, sine
    )
    square = (drafts, drafts)
    draft_valid = (depth_along[0] < depth_down[...]) | (
        lax.broadcasted_iota(jnp.int32, square, 0) == lax.broadcasted_iota(jnp.int32, square, 1)
    )
    draft_k = draft_kv[:, 0, :]
    draft_v = draft_kv[:, 1, :]
    for h in range(raw.shape[1] // head_dim):
        lanes = slice(h * head_dim, (h + 1) * head_dim)
        query = raw[:, lanes]
        swapped = jnp.concatenate(
            [query[:, head_dim // 2 :], query[:, : head_dim // 2]], axis=1
        )
        query = query * cosine + swapped * sine
        query = (query * head_dim ** (-0.5)).astype(jnp.bfloat16)
        cache = lax.dot_general(query, keys[request], both, preferred_element_type=f32)
        cache = jnp.where(valid, cache, -jnp.inf)
        draft = lax.dot_general(query, draft_k, both, preferred_element_type=f32)
        draft = jnp.where(draft_valid, draft, -jnp.inf)
        peak = jnp.maximum(
            jnp.max(cache, axis=-1, keepdims=True), jnp.max(draft, axis=-1, keepdims=True)
        )
        cache = jnp.exp(cache - peak)
        draft = jnp.exp(draft - peak)
        share = 1.0 / (
            jnp.sum(cache, axis=-1, keepdims=True) + jnp.sum(draft, axis=-1, keepdims=True)
        )
        cache = (cache * share).astype(jnp.bfloat16)
        draft = (draft * share).astype(jnp.bfloat16)
        rows = jnp.dot(cache, values[request], preferred_element_type=f32)
        rows = rows + jnp.dot(draft, draft_v, preferred_element_type=f32)
        out[:, lanes] = rows.astype(out.dtype)


def attention(raw, depth, frequency, draft_kv, blocks, table, lengths, head):
    rows, columns = raw.shape
    requests, listed = table.shape
    drafts = rows // requests
    block_len, head_dim = blocks.shape[2:]
    context = listed * block_len

    def by_rows(width):
        return pl.BlockSpec((drafts, width), lambda r, *_: (r, 0))

    return pl.pallas_call(
        attention_kernel,
        out_shape=jax.ShapeDtypeStruct((rows, columns), jnp.bfloat16),
        grid_spec=pltpu.PrefetchScalarGridSpec(
            num_scalar_prefetch=3,
            grid=(requests,),
            in_specs=[
                by_rows(columns),
                by_rows(1),
                pl.BlockSpec((1, 1, drafts), lambda r, *_: (r, 0, 0)),
                pl.BlockSpec((1, head_dim), lambda r, *_: (0, 0)),
                pl.BlockSpec((drafts, 2, head_dim), lambda r, table, lengths, head: (r, 0, head[0])),
                pl.BlockSpec(memory_space=pl.ANY),
            ],
            out_specs=by_rows(columns),
            scratch_shapes=[
                pltpu.VMEM((requests, context, head_dim), blocks.dtype),
                pltpu.VMEM((requests, context, head_dim), blocks.dtype),
                pltpu.SemaphoreType.DMA((2, requests, listed)),
            ],
        ),
        compiler_params=pltpu.CompilerParams(
            dimension_semantics=("arbitrary",), vmem_limit_bytes=VMEM_LIMIT
        ),
        name="mid",
    )(
        table, lengths, head, raw, depth.reshape(rows, 1), depth[:, None, :], frequency,
        draft_kv, blocks,
    )


def shards(
    hidden, norm_gain, w_query, w_out, kv_pool, draft_kv, block_table, cached_len, draft_pos
):
    nt = lax.axis_size("tensor")
    ny = 2 if nt == 8 else 1
    devices = lax.axis_size(("pool", "tensor"))
    my_rank = lax.axis_index(("pool", "tensor"))
    kv_heads = kv_pool.shape[1]
    block_len = kv_pool.shape[3]
    head_dim = kv_pool.shape[4]
    group_size = devices // kv_heads
    own_head = my_rank // group_size
    gain = norm_gain.reshape(1, -1)
    raw_queries, arrived, w_mate = front(
        ny, nt, group_size, hidden, gain, kv_pool, w_out, w_query
    )
    half = np.arange(head_dim // 2, dtype=np.float64)
    frequency = np.tile(500000.0 ** (-2.0 * half / head_dim), 2).astype(np.float32)
    blocks = arrived.reshape(-1, 2, block_len, head_dim)
    heads_out = attention(
        raw_queries, draft_pos, jnp.asarray(frequency)[None, :], draft_kv, blocks,
        block_table, cached_len, jnp.reshape(own_head, (1,)),
    )
    return back(ny, nt, heads_out, w_out, w_mate)


def solution(mesh):
    placed = (
        P("groups", ("pool", "tensor")),
        P(),
        P(None, ("pool", "tensor")),
        P(("pool", "tensor"), None),
        P(("groups", "pool", "tensor"), None, None, None, None),
        P("groups", None, None),
        P("groups", None),
        P("groups"),
        P("groups", None),
    )
    return jax.shard_map(
        shards, mesh=mesh, in_specs=placed, out_specs=P("groups", None), check_vma=False
    )
```

```python
import functools

import jax
import jax.numpy as jnp
import numpy as np
from jax import lax
from jax.experimental import pallas as pl
from jax.experimental.pallas import tpu as pltpu
from jax.sharding import PartitionSpec as P

VMEM_LIMIT = 24 * 1024 * 1024
FRONT_VMEM_LIMIT = 56 * 1024 * 1024
PIECES = 2


class Place:
    def __init__(self, ny, nt):
        self.ny, self.nz, self.nt = ny, nt // ny, nt
        self.p = lax.axis_index("pool")
        self.t = lax.axis_index("tensor")
        self.y = lax.rem(self.t, ny)
        self.z = self.t // ny

    def chip(self, z, y):
        return z * self.ny + y

    def up(self, z, by):
        return lax.rem(z + by, self.nz)

    def down(self, z, by):
        return lax.rem(z + self.nz - by, self.nz)

    def rank(self, p, t):
        return p * self.nt + t

    @property
    def mate(self):
        return {"pool": 1 - self.p, "tensor": self.t}

    @property
    def across(self):
        return {"pool": self.p, "tensor": self.chip(self.z, 1 - self.y)}

    @property
    def next(self):
        return {"pool": self.p, "tensor": self.chip(self.up(self.z, 1), self.y)}

    @property
    def previous(self):
        return {"pool": self.p, "tensor": self.chip(self.down(self.z, 1), self.y)}


def remote(src, dst, send, recv, device):
    return pltpu.make_async_remote_copy(
        src_ref=src,
        dst_ref=dst,
        send_sem=send,
        recv_sem=recv,
        device_id=device,
        device_id_type=pl.DeviceIdType.MESH,
    )


def meet(devices):
    barrier = pltpu.get_barrier_semaphore()
    for device in devices:
        pl.semaphore_signal(barrier, inc=1, device_id=device, device_id_type=pl.DeviceIdType.MESH)
    pl.semaphore_wait(barrier, len(devices))


def gather_blocks(at, own, block_of, sems, use=None, keep_last=False):
    zs, zr, ys, yr, ms, mr, ls = sems
    nz, ny = at.nz, at.ny
    part = own.shape[0] // PIECES

    def rows(ref, h):
        return ref.at[pl.ds(h * part, part), :]

    def block(p, z, y, h):
        return rows(block_of(at.rank(p, at.chip(z, y))), h)

    if keep_last:
        keep = pltpu.make_async_copy(own, block_of(at.rank(at.p, at.t)), ls)
    started = []

    def send(src, dst, send_sem, recv_sem, device):
        started.append(remote(src, dst, send_sem, recv_sem, device))
        started[-1].start()

    def ring(s, h):
        z = at.down(at.z, s)
        here = block(at.p, z, at.y, h)
        src = rows(own, h) if s == 0 else here
        if s > 0:
            remote(here, here, zs.at[s - 1, h], zr.at[s - 1, h], at.previous).wait_recv()
        if s < nz - 1:
            send(src, here, zs.at[s, h], zr.at[s, h], at.next)
        if ny == 2:
            send(src, here, ys.at[s, h], yr.at[s, h], at.across)
        send(src, here, ms.at[s, h], mr.at[s, h], at.mate)

    def from_across(s, h):
        if ny == 2:
            there = block(at.p, at.down(at.z, s), 1 - at.y, h)
            remote(there, there, ys.at[s, h], yr.at[s, h], at.across).wait_recv()
            send(there, there, ms.at[nz + s, h], mr.at[nz + s, h], at.mate)

    def step(s, pieces=range(PIECES)):
        for h in pieces:
            if s < nz:
                ring(s, h)
            if s > 0:
                from_across(s - 1, h)
            if keep_last and s == 0 and h == PIECES - 1:
                keep.start()

    def arrive(s):
        z = at.down(at.z, s)
        for y_at in range(ny):
            y = at.y if y_at == 0 else 1 - at.y
            slot = s + y_at * nz
            if use is not None and s + y_at > 0:
                use(at.rank(at.p, at.chip(z, y)))
            for h in range(PIECES):
                there = block(1 - at.p, z, y, h)
                remote(there, there, ms.at[slot, h], mr.at[slot, h], at.mate).wait_recv()
            if use is not None:
                use(at.rank(1 - at.p, at.chip(z, y)))

    def finish():
        for copy in started:
            copy.wait_send()
        if keep_last:
            keep.wait()

    return step, arrive, finish


def gather_sems(ny, nz):
    dma = pltpu.SemaphoreType.DMA
    once, twice = dma((nz, PIECES)), dma((2 * nz, PIECES))
    return [once, once, once, once, twice, twice, dma]


def front_kernel(
    ny, nt, group_size, hidden, gain, kv, w_out, w_query, raw, blocks, w_mate,
    squares, squares_all, scales, normed, gathered, w_buf,
    zs, zr, ys, yr, ms, mr, ls, ks, kr, fs, fr, ws, wr, bs, w_sem, ss, sr,
):
    at = Place(ny, nt)
    nz = at.nz
    ranks = 2 * nt
    width = hidden.shape[1]

    def load(rank):
        start = pl.multiple_of(rank * width, width)
        return pltpu.make_async_copy(
            w_query.at[pl.ds(start, width), :], w_buf.at[rank], w_sem.at[rank]
        )

    def start_load(rank, carry):
        load(rank).start()
        return carry

    lax.fori_loop(0, ranks, start_load, 0)
    others = []
    for dt in range(nt):
        for dp in range(2):
            if dt + dp > 0:
                others.append({"pool": lax.rem(at.p + dp, 2), "tensor": lax.rem(at.t + dt, nt)})
    meet(others)
    me = at.rank(at.p, at.t)
    step, arrive, finish = gather_blocks(
        at, hidden, lambda rank: gathered.at[rank], (zs, zr, ys, yr, ms, mr, ls),
        lambda rank: use(rank),
    )
    step(0)

    wide = hidden[...].astype(jnp.float32)
    squares[...] = lax.dot_general(
        jnp.ones((8, width), jnp.float32), wide * wide, (((1,), (1,)), ((), ())),
        precision=lax.Precision.HIGHEST, preferred_element_type=jnp.float32,
    )
    square_copies = [
        remote(squares, squares_all.at[i], ss.at[i], sr.at[i], device)
        for i, device in enumerate(others)
    ]
    for copy in square_copies:
        copy.start()

    def head_of(p, t):
        return at.rank(p, t) // group_size

    keep = pltpu.make_async_copy(kv.at[:, head_of(at.p, at.t)], blocks.at[me], bs)
    keep.start()
    half = w_mate.shape[1]
    swap = remote(
        w_out.at[:, pl.ds(pl.multiple_of((1 - at.p) * half, half), half)],
        w_mate, ws, wr, at.mate,
    )
    sends = []

    def send_blocks(dz):
        for dp in range(2):
            if dz + dp > 0:
                device = {
                    "pool": lax.rem(at.p + dp, 2),
                    "tensor": at.chip(at.up(at.z, dz), at.y),
                }
                slot = dz * 2 + dp
                head = head_of(device["pool"], device["tensor"])
                sends.append(remote(kv.at[:, head], blocks.at[me], ks.at[slot], kr.at[slot], device))
                sends[-1].start()

    send_blocks(0)

    def use(rank):
        load(rank).wait()
        start = pl.multiple_of(rank * width, width)
        for c in range(width // 128):
            lanes = slice(c * 128, (c + 1) * 128)
            features = pl.ds(pl.multiple_of(start + c * 128, 128), 128)
            normed[:, lanes] = (
                gathered[rank, :, lanes].astype(jnp.float32) * scales[...] * gain[:, features]
            ).astype(normed.dtype)
        raw[...] += jnp.dot(normed[...], w_buf[rank], preferred_element_type=jnp.float32)

    def sum_squares():
        total = squares[...]
        for i, copy in enumerate(square_copies):
            copy.wait_recv()
            total = total + squares_all[i]
        scale = lax.rsqrt(total * (1.0 / (width * ranks)) + 1e-05)
        scales[...] = jnp.transpose(jnp.concatenate([scale] * 16, axis=0))

    def block_from(dz, dp):
        return at.rank(lax.rem(at.p + dp, 2), at.chip(at.down(at.z, dz), at.y))

    def forward(dz):
        for dp in range(2):
            slot = dz * 2 + dp
            here = blocks.at[block_from(dz, dp)]
            src = here
            if slot == 0:
                src = kv.at[:, head_of(at.p, at.t)]
            else:
                remote(here, here, ks.at[slot], kr.at[slot], at.mate).wait_recv()
            if ny == 2:
                sends.append(remote(src, here, fs.at[slot], fr.at[slot], at.across))
                sends[-1].start()

    forward(0)
    swap.start()
    gathered[me] = hidden[...]
    raw[...] = jnp.zeros_like(raw)
    sum_squares()
    use(me)
    for s in range(1, nz + 1):
        step(s)
        if s < nz:
            send_blocks(s)
        if s > 1:
            forward(s - 1)
        arrive(s - 1)
    finish()
    if ny == 2:
        for dz in range(nz):
            for dp in range(2):
                slot = dz * 2 + dp
                source = at.rank(
                    lax.rem(at.p + dp, 2), at.chip(at.down(at.z, dz), 1 - at.y)
                )
                there = blocks.at[source]
                remote(there, there, fs.at[slot], fr.at[slot], at.across).wait_recv()
    for copy in sends + square_copies:
        copy.wait_send()
    swap.wait()
    keep.wait()


def front(ny, nt, group_size, hidden, gain, kv_pool, w_out, w_query):
    rows, width = hidden.shape
    columns = w_query.shape[1]
    nz = nt // ny
    ranks = 2 * nt
    dma = pltpu.SemaphoreType.DMA
    blocks = (ranks, kv_pool.shape[0]) + kv_pool.shape[2:]
    return pl.pallas_call(
        functools.partial(front_kernel, ny, nt, group_size),
        out_shape=(
            jax.ShapeDtypeStruct((rows, columns), jnp.float32),
            jax.ShapeDtypeStruct(blocks, kv_pool.dtype),
            jax.ShapeDtypeStruct((w_out.shape[0], w_out.shape[1] // 2), w_out.dtype),
        ),
        in_specs=[pl.BlockSpec(memory_space=pltpu.VMEM)] * 2
        + [pl.BlockSpec(memory_space=pl.ANY)] * 3,
        out_specs=(
            pl.BlockSpec(memory_space=pltpu.VMEM),
            pl.BlockSpec(memory_space=pl.ANY),
            pl.BlockSpec(memory_space=pl.ANY),
        ),
        scratch_shapes=[
            pltpu.VMEM((8, rows), jnp.float32),
            pltpu.VMEM((ranks - 1, 8, rows), jnp.float32),
            pltpu.VMEM((rows, 128), jnp.float32),
            pltpu.VMEM((rows, width), hidden.dtype),
            pltpu.VMEM((ranks, rows, width), hidden.dtype),
            pltpu.VMEM((ranks, width, columns), w_query.dtype),
        ]
        + gather_sems(ny, nz)
        + [dma((2 * nz,)), dma((2 * nz,)), dma((2 * nz,)), dma((2 * nz,)), dma, dma, dma]
        + [dma((ranks,)), dma((ranks - 1,)), dma((ranks - 1,))],
        compiler_params=pltpu.CompilerParams(
            collective_id=0, has_side_effects=True, vmem_limit_bytes=FRONT_VMEM_LIMIT
        ),
        name="front",
    )(hidden, gain, kv_pool, w_out, w_query)


def code(value, codes, scales):
    peak = jnp.maximum(jnp.max(jnp.abs(value), axis=0, keepdims=True), 1e-30)
    codes[...] = jnp.round(value * (32767.0 / peak)).astype(jnp.int32).astype(jnp.int16)
    scales[...] = jnp.broadcast_to(peak * (1.0 / 32767.0), scales.shape)


def decode(codes, scales):
    return codes[...].astype(jnp.int32).astype(jnp.float32) * scales[0:1, :]


def back_kernel(
    ny, nt, heads, w_own, w_mate, out,
    heads_mate, w_buf, y_send, y_recv, z_send, z_recv,
    y_send_scale, y_recv_scale, z_send_scale, z_recv_scale, final,
    hs, hr, w_sem, ps, pr, qs, qr, pss, psr, qss, qsr, zs, zr, ys, yr, ms, mr, ls,
):
    at = Place(ny, nt)
    nz = at.nz
    width = final.shape[1]
    half = w_mate.shape[1]

    def load(which, t):
        if which == 0:
            start = pl.multiple_of(at.p * half + t * width, width)
            src = w_own.at[:, pl.ds(start, width)]
        else:
            src = w_mate.at[:, pl.ds(pl.multiple_of(t * width, width), width)]
        return pltpu.make_async_copy(src, w_buf.at[which, t], w_sem.at[which, t])

    part = heads.shape[0] // PIECES

    def chip_of(s, y):
        return at.chip(lax.rem(at.z + 2 * nz - 1 - s, nz), y)

    def start_loads(y):
        def body(s, carry):
            t = chip_of(s, y)
            load(0, t).start()
            load(1, t).start()
            return carry

        lax.fori_loop(0, nz, body, 0)

    if ny == 2:
        start_loads(1 - at.y)
    start_loads(at.y)
    neighbours = [at.mate, at.next, at.previous] + ([at.across] if ny == 2 else [])
    meet(neighbours)
    trade = remote(heads, heads_mate, hs, hr, at.mate)
    trade.start()
    trade.wait()

    def rows_of(i):
        return pl.ds(pl.multiple_of(lax.rem(i, PIECES) * part, part), part)

    def wait_loads(y):
        def body(s, carry):
            t = chip_of(s, y)
            load(0, t).wait()
            load(1, t).wait()
            return carry

        lax.fori_loop(0, nz, body, 0)

    def term(i, y):
        t = chip_of(i // PIECES, y)
        return jnp.dot(
            heads[rows_of(i), :], w_buf[0, t], preferred_element_type=jnp.float32
        ) + jnp.dot(heads_mate[rows_of(i), :], w_buf[1, t], preferred_element_type=jnp.float32)

    def across_copies(i):
        return [
            remote(y_send.at[i], y_recv.at[i], ps.at[i], pr.at[i], at.across),
            remote(y_send_scale.at[i], y_recv_scale.at[i], pss.at[i], psr.at[i], at.across),
        ]

    def ring_copies(i):
        return [
            remote(z_send.at[i], z_recv.at[i], qs.at[i], qr.at[i], at.next),
            remote(z_send_scale.at[i], z_recv_scale.at[i], qss.at[i], qsr.at[i], at.next),
        ]

    if ny == 2:
        wait_loads(1 - at.y)

        def send_across(i, carry):
            code(term(i, 1 - at.y), y_send.at[i], y_send_scale.at[i])
            for copy in across_copies(i):
                copy.start()
            return carry

        lax.fori_loop(0, nz * PIECES, send_across, 0)
    wait_loads(at.y)

    def total(i):
        value = term(i, at.y)
        if ny == 2:
            for copy in across_copies(i):
                copy.wait_recv()
            value = value + decode(y_recv.at[i], y_recv_scale.at[i])
        return value

    def ring_received(i):
        for copy in ring_copies(i):
            copy.wait_recv()
        return decode(z_recv.at[i], z_recv_scale.at[i])

    def ring_send(i, value):
        code(value, z_send.at[i], z_send_scale.at[i])
        for copy in ring_copies(i):
            copy.start()

    def ring_first(i, carry):
        ring_send(i, total(i))
        return carry

    lax.fori_loop(0, PIECES, ring_first, 0)

    def ring_step(i, carry):
        value = total(i)
        ring_send(i, value + ring_received(i - PIECES))
        return carry

    lax.fori_loop(PIECES, (nz - 1) * PIECES, ring_step, 0)

    def block_of(rank):
        return out.at[:, pl.ds(pl.multiple_of(rank * width, width), width)]

    step, arrive, finish = gather_blocks(
        at, final, block_of, (zs, zr, ys, yr, ms, mr, ls), keep_last=True
    )
    for h in range(PIECES):
        i = (nz - 1) * PIECES + h
        value = total(i)
        final[h * part : (h + 1) * part, :] = (value + ring_received(i - PIECES)).astype(
            final.dtype
        )
        step(0, (h,))
    for s in range(1, nz + 1):
        step(s)
    for s in range(nz):
        arrive(s)
    finish()

    def sent(i, carry):
        if ny == 2:
            for copy in across_copies(i):
                copy.wait_send()
        return carry

    lax.fori_loop(0, nz * PIECES, sent, 0)

    def ring_sent(s, carry):
        for copy in ring_copies(s):
            copy.wait_send()
        return carry

    lax.fori_loop(0, (nz - 1) * PIECES, ring_sent, 0)


def back(ny, nt, heads, w_out, w_mate):
    rows, depth = heads.shape
    columns = w_out.shape[1]
    nz = nt // ny
    width = columns // (2 * nt)
    dma = pltpu.SemaphoreType.DMA
    f32 = jnp.float32
    return pl.pallas_call(
        functools.partial(back_kernel, ny, nt),
        out_shape=jax.ShapeDtypeStruct((rows, columns), jnp.bfloat16),
        in_specs=[
            pl.BlockSpec(memory_space=pltpu.VMEM),
            pl.BlockSpec(memory_space=pl.ANY),
            pl.BlockSpec(memory_space=pl.ANY),
        ],
        out_specs=pl.BlockSpec(memory_space=pl.ANY),
        scratch_shapes=[
            pltpu.VMEM((rows, depth), heads.dtype),
            pltpu.VMEM((2, nt, depth, width), w_out.dtype),
            pltpu.VMEM((nz * PIECES, rows // PIECES, width), jnp.int16),
            pltpu.VMEM((nz * PIECES, rows // PIECES, width), jnp.int16),
            pltpu.VMEM(((nz - 1) * PIECES, rows // PIECES, width), jnp.int16),
            pltpu.VMEM(((nz - 1) * PIECES, rows // PIECES, width), jnp.int16),
            pltpu.VMEM((nz * PIECES, 8, width), f32),
            pltpu.VMEM((nz * PIECES, 8, width), f32),
            pltpu.VMEM(((nz - 1) * PIECES, 8, width), f32),
            pltpu.VMEM(((nz - 1) * PIECES, 8, width), f32),
            pltpu.VMEM((rows, width), jnp.bfloat16),
            dma,
            dma,
            dma((2, nt)),
            dma((nz * PIECES,)),
            dma((nz * PIECES,)),
            dma((nz * PIECES,)),
            dma((nz * PIECES,)),
            dma((nz * PIECES,)),
            dma((nz * PIECES,)),
            dma((nz * PIECES,)),
            dma((nz * PIECES,)),
        ]
        + gather_sems(ny, nz),
        compiler_params=pltpu.CompilerParams(
            collective_id=1, has_side_effects=True, vmem_limit_bytes=VMEM_LIMIT
        ),
        name="back",
    )(heads, w_out, w_mate)


def attention_kernel(
    table, lengths, head, raw, depth_down, depth_along, frequency, draft_kv, blocks, out, keys, values, sems
):
    request = pl.program_id(0)
    requests, context, head_dim = keys.shape
    block_len = blocks.shape[2]
    listed = context // block_len

    def copies(r, j):
        here = pl.ds(pl.multiple_of(j * block_len, block_len), block_len)
        block = table[r, j]
        return [
            pltpu.make_async_copy(blocks.at[block, 0], keys.at[r, here, :], sems.at[0, r, j]),
            pltpu.make_async_copy(blocks.at[block, 1], values.at[r, here, :], sems.at[1, r, j]),
        ]

    @pl.when(request == 0)
    def _():
        def start(i, carry):
            for copy in copies(i // listed, lax.rem(i, listed)):
                copy.start()
            return carry

        lax.fori_loop(0, requests * listed, start, 0)

    def arrived(j, carry):
        for copy in copies(request, j):
            copy.wait()
        return carry

    lax.fori_loop(0, listed, arrived, 0)
    both = (((1,), (1,)), ((), ()))
    f32 = jnp.float32
    valid = lax.broadcasted_iota(jnp.int32, (1, context), 1) < lengths[request]
    drafts = raw.shape[0]
    angles = (lengths[request] + depth_down[...]).astype(f32) * frequency[...]
    cosine = jnp.cos(angles)
    sine = jnp.sin(angles)
    sine = jnp.where(
        lax.broadcasted_iota(jnp.int32, (1, head_dim), 1) < head_dim // 2, -sine, sine
    )
    square = (drafts, drafts)
    draft_valid = (depth_along[0] < depth_down[...]) | (
        lax.broadcasted_iota(jnp.int32, square, 0) == lax.broadcasted_iota(jnp.int32, square, 1)
    )
    draft_k = draft_kv[:, 0, :]
    draft_v = draft_kv[:, 1, :]
    heads = raw.shape[1] // head_dim
    queries = []
    for h in range(heads):
        query = raw[:, h * head_dim : (h + 1) * head_dim]
        swapped = jnp.concatenate(
            [query[:, head_dim // 2 :], query[:, : head_dim // 2]], axis=1
        )
        query = query * cosine + swapped * sine
        queries.append((query * head_dim ** (-0.5)).astype(jnp.bfloat16))
    query = jnp.concatenate(queries, axis=0)
    cache = lax.dot_general(query, keys[request], both, preferred_element_type=f32)
    cache = jnp.where(valid, cache, -jnp.inf)
    draft = lax.dot_general(query, draft_k, both, preferred_element_type=f32)
    draft = jnp.concatenate(
        [
            jnp.where(draft_valid, draft[h * drafts : (h + 1) * drafts, :], -jnp.inf)
            for h in range(heads)
        ],
        axis=0,
    )
    peak = jnp.maximum(
        jnp.max(cache, axis=-1, keepdims=True), jnp.max(draft, axis=-1, keepdims=True)
    )
    cache = jnp.exp(cache - peak)
    draft = jnp.exp(draft - peak)
    share = 1.0 / (
        jnp.sum(cache, axis=-1, keepdims=True) + jnp.sum(draft, axis=-1, keepdims=True)
    )
    cache = (cache * share).astype(jnp.bfloat16)
    draft = (draft * share).astype(jnp.bfloat16)
    rows = jnp.dot(cache, values[request], preferred_element_type=f32)
    rows = rows + jnp.dot(draft, draft_v, preferred_element_type=f32)
    for h in range(heads):
        out[:, h * head_dim : (h + 1) * head_dim] = rows[
            h * drafts : (h + 1) * drafts, :
        ].astype(out.dtype)


def attention(raw, depth, frequency, draft_kv, blocks, table, lengths, head):
    rows, columns = raw.shape
    requests, listed = table.shape
    drafts = rows // requests
    block_len, head_dim = blocks.shape[2:]
    context = listed * block_len

    def by_rows(width):
        return pl.BlockSpec((drafts, width), lambda r, *_: (r, 0))

    return pl.pallas_call(
        attention_kernel,
        out_shape=jax.ShapeDtypeStruct((rows, columns), jnp.bfloat16),
        grid_spec=pltpu.PrefetchScalarGridSpec(
            num_scalar_prefetch=3,
            grid=(requests,),
            in_specs=[
                by_rows(columns),
                by_rows(1),
                pl.BlockSpec((1, 1, drafts), lambda r, *_: (r, 0, 0)),
                pl.BlockSpec((1, head_dim), lambda r, *_: (0, 0)),
                pl.BlockSpec((drafts, 2, head_dim), lambda r, table, lengths, head: (r, 0, head[0])),
                pl.BlockSpec(memory_space=pl.ANY),
            ],
            out_specs=by_rows(columns),
            scratch_shapes=[
                pltpu.VMEM((requests, context, head_dim), blocks.dtype),
                pltpu.VMEM((requests, context, head_dim), blocks.dtype),
                pltpu.SemaphoreType.DMA((2, requests, listed)),
            ],
        ),
        compiler_params=pltpu.CompilerParams(
            dimension_semantics=("arbitrary",), vmem_limit_bytes=VMEM_LIMIT
        ),
        name="mid",
    )(
        table, lengths, head, raw, depth.reshape(rows, 1), depth[:, None, :], frequency,
        draft_kv, blocks,
    )


def shards(
    hidden, norm_gain, w_query, w_out, kv_pool, draft_kv, block_table, cached_len, draft_pos
):
    nt = lax.axis_size("tensor")
    ny = 2 if nt == 8 else 1
    devices = lax.axis_size(("pool", "tensor"))
    my_rank = lax.axis_index(("pool", "tensor"))
    kv_heads = kv_pool.shape[1]
    block_len = kv_pool.shape[3]
    head_dim = kv_pool.shape[4]
    group_size = devices // kv_heads
    own_head = my_rank // group_size
    gain = norm_gain.reshape(1, -1)
    raw_queries, arrived, w_mate = front(
        ny, nt, group_size, hidden, gain, kv_pool, w_out, w_query
    )
    half = np.arange(head_dim // 2, dtype=np.float64)
    frequency = np.tile(500000.0 ** (-2.0 * half / head_dim), 2).astype(np.float32)
    blocks = arrived.reshape(-1, 2, block_len, head_dim)
    heads_out = attention(
        raw_queries, draft_pos, jnp.asarray(frequency)[None, :], draft_kv, blocks,
        block_table, cached_len, jnp.reshape(own_head, (1,)),
    )
    return back(ny, nt, heads_out, w_out, w_mate)


def solution(mesh):
    placed = (
        P("groups", ("pool", "tensor")),
        P(),
        P(None, ("pool", "tensor")),
        P(("pool", "tensor"), None),
        P(("groups", "pool", "tensor"), None, None, None, None),
        P("groups", None, None),
        P("groups", None),
        P("groups"),
        P("groups", None),
    )
    return jax.shard_map(
        shards, mesh=mesh, in_specs=placed, out_specs=P("groups", None), check_vma=False
    )
```

```python
import functools

import jax
import jax.numpy as jnp
import numpy as np
from jax import lax
from jax.experimental import pallas as pl
from jax.experimental.pallas import tpu as pltpu
from jax.sharding import PartitionSpec as P

VMEM_LIMIT = 40 * 1024 * 1024
WIDE_VMEM_LIMIT = 56 * 1024 * 1024
PIECES = 2


class Place:
    def __init__(self, ny, nt):
        self.ny, self.nz, self.nt = ny, nt // ny, nt
        self.p = lax.axis_index("pool")
        self.t = lax.axis_index("tensor")
        self.y = lax.rem(self.t, ny)
        self.z = self.t // ny

    def chip(self, z, y):
        return z * self.ny + y

    def up(self, z, by):
        return lax.rem(z + by, self.nz)

    def down(self, z, by):
        return lax.rem(z + self.nz - by, self.nz)

    def rank(self, p, t):
        return p * self.nt + t

    @property
    def mate(self):
        return {"pool": 1 - self.p, "tensor": self.t}

    @property
    def across(self):
        return {"pool": self.p, "tensor": self.chip(self.z, 1 - self.y)}

    @property
    def next(self):
        return {"pool": self.p, "tensor": self.chip(self.up(self.z, 1), self.y)}

    @property
    def previous(self):
        return {"pool": self.p, "tensor": self.chip(self.down(self.z, 1), self.y)}


def remote(src, dst, send, recv, device):
    return pltpu.make_async_remote_copy(
        src_ref=src,
        dst_ref=dst,
        send_sem=send,
        recv_sem=recv,
        device_id=device,
        device_id_type=pl.DeviceIdType.MESH,
    )


def meet(devices):
    barrier = pltpu.get_barrier_semaphore()
    for device in devices:
        pl.semaphore_signal(barrier, inc=1, device_id=device, device_id_type=pl.DeviceIdType.MESH)
    pl.semaphore_wait(barrier, len(devices))


def gather_blocks(at, own, block_of, sems, use=None, keep_last=False):
    zs, zr, ys, yr, ms, mr, ls = sems
    nz, ny = at.nz, at.ny
    part = own.shape[0] // PIECES

    def rows(ref, h):
        return ref.at[pl.ds(h * part, part), :]

    def block(p, z, y, h):
        return rows(block_of(at.rank(p, at.chip(z, y))), h)

    if keep_last:
        keep = pltpu.make_async_copy(own, block_of(at.rank(at.p, at.t)), ls)
    started = []

    def send(src, dst, send_sem, recv_sem, device):
        started.append(remote(src, dst, send_sem, recv_sem, device))
        started[-1].start()

    def ring(s, h):
        z = at.down(at.z, s)
        here = block(at.p, z, at.y, h)
        src = rows(own, h) if s == 0 else here
        if s > 0:
            remote(here, here, zs.at[s - 1, h], zr.at[s - 1, h], at.previous).wait_recv()
        if s < nz - 2:
            send(src, here, zs.at[s, h], zr.at[s, h], at.next)
        if s == 0:
            send(src, here, zs.at[nz - 2, h], zr.at[nz - 2, h], at.previous)
        if ny == 2 and s < nz - 1:
            send(src, here, ys.at[s, h], yr.at[s, h], at.across)
        send(src, here, ms.at[s, h], mr.at[s, h], at.mate)

    def from_across(s, h):
        if ny == 2:
            there = block(at.p, at.down(at.z, s), 1 - at.y, h)
            remote(there, there, ys.at[s, h], yr.at[s, h], at.across).wait_recv()
            if s == 0:
                send(there, there, ys.at[nz - 1, h], yr.at[nz - 1, h], at.previous)
            send(there, there, ms.at[nz + s, h], mr.at[nz + s, h], at.mate)

    def step(s, pieces=range(PIECES)):
        for h in pieces:
            if s < nz:
                ring(s, h)
            if s > 0:
                from_across(s - 1, h)
            if keep_last and s == 0 and h == PIECES - 1:
                keep.start()

    def arrive(s):
        z = at.down(at.z, s)
        for y_at in range(ny):
            y = at.y if y_at == 0 else 1 - at.y
            slot = s + y_at * nz
            if use is not None and s + y_at > 0:
                use(at.rank(at.p, at.chip(z, y)))
            for h in range(PIECES):
                there = block(1 - at.p, z, y, h)
                remote(there, there, ms.at[slot, h], mr.at[slot, h], at.mate).wait_recv()
            if use is not None:
                use(at.rank(1 - at.p, at.chip(z, y)))

    def finish():
        for copy in started:
            copy.wait_send()
        if keep_last:
            keep.wait()

    return step, arrive, finish


def gather_sems(ny, nz):
    dma = pltpu.SemaphoreType.DMA
    once, twice = dma((nz, PIECES)), dma((2 * nz, PIECES))
    return [once, once, once, once, twice, twice, dma]


def front_kernel(
    ny, nt, group_size, hidden, gain, kv, w_out, w_query, raw, blocks, w_mate,
    squares, squares_all, scales, normed, gathered, w_buf,
    zs, zr, ys, yr, ms, mr, ls, ks, kr, fs, fr, ws, wr, bs, w_sem, ss, sr,
):
    at = Place(ny, nt)
    nz = at.nz
    ranks = 2 * nt
    width = hidden.shape[1]

    def load(rank):
        start = pl.multiple_of(rank * width, width)
        return pltpu.make_async_copy(
            w_query.at[pl.ds(start, width), :], w_buf.at[rank], w_sem.at[rank]
        )

    def start_load(rank, carry):
        load(rank).start()
        return carry

    lax.fori_loop(0, ranks, start_load, 0)
    others = []
    for dt in range(nt):
        for dp in range(2):
            if dt + dp > 0:
                others.append({"pool": lax.rem(at.p + dp, 2), "tensor": lax.rem(at.t + dt, nt)})
    meet(others)
    me = at.rank(at.p, at.t)
    step, arrive, finish = gather_blocks(
        at, hidden, lambda rank: gathered.at[rank], (zs, zr, ys, yr, ms, mr, ls),
        lambda rank: use(rank),
    )
    step(0)

    wide = hidden[...].astype(jnp.float32)
    squares[...] = lax.dot_general(
        jnp.ones((8, width), jnp.float32), wide * wide, (((1,), (1,)), ((), ())),
        precision=lax.Precision.HIGHEST, preferred_element_type=jnp.float32,
    )
    square_copies = [
        remote(squares, squares_all.at[i], ss.at[i], sr.at[i], device)
        for i, device in enumerate(others)
    ]
    for copy in square_copies:
        copy.start()

    def head_of(p, t):
        return at.rank(p, t) // group_size

    keep = pltpu.make_async_copy(kv.at[:, head_of(at.p, at.t)], blocks.at[me], bs)
    keep.start()
    half = w_mate.shape[1]
    swap = remote(
        w_out.at[:, pl.ds(pl.multiple_of((1 - at.p) * half, half), half)],
        w_mate, ws, wr, at.mate,
    )
    sends = []

    def send_blocks(dz):
        for dp in range(2):
            if dz + dp > 0:
                device = {
                    "pool": lax.rem(at.p + dp, 2),
                    "tensor": at.chip(at.up(at.z, dz), at.y),
                }
                slot = dz * 2 + dp
                head = head_of(device["pool"], device["tensor"])
                sends.append(remote(kv.at[:, head], blocks.at[me], ks.at[slot], kr.at[slot], device))
                sends[-1].start()

    send_blocks(0)

    def use(rank):
        load(rank).wait()
        start = pl.multiple_of(rank * width, width)
        for c in range(width // 128):
            lanes = slice(c * 128, (c + 1) * 128)
            features = pl.ds(pl.multiple_of(start + c * 128, 128), 128)
            normed[:, lanes] = (
                gathered[rank, :, lanes].astype(jnp.float32) * scales[...] * gain[:, features]
            ).astype(normed.dtype)
        raw[...] += jnp.dot(normed[...], w_buf[rank], preferred_element_type=jnp.float32)

    def sum_squares():
        total = squares[...]
        for i, copy in enumerate(square_copies):
            copy.wait_recv()
            total = total + squares_all[i]
        scale = lax.rsqrt(total * (1.0 / (width * ranks)) + 1e-05)
        scales[...] = jnp.transpose(jnp.concatenate([scale] * 16, axis=0))

    def block_from(dz, dp):
        return at.rank(lax.rem(at.p + dp, 2), at.chip(at.down(at.z, dz), at.y))

    def forward(dz):
        for dp in range(2):
            slot = dz * 2 + dp
            here = blocks.at[block_from(dz, dp)]
            src = here
            if slot == 0:
                src = kv.at[:, head_of(at.p, at.t)]
            else:
                remote(here, here, ks.at[slot], kr.at[slot], at.mate).wait_recv()
            if ny == 2:
                sends.append(remote(src, here, fs.at[slot], fr.at[slot], at.across))
                sends[-1].start()

    forward(0)
    swap.start()
    gathered[me] = hidden[...]
    raw[...] = jnp.zeros_like(raw)
    sum_squares()
    use(me)
    for s in range(1, nz + 1):
        step(s)
        if s < nz:
            send_blocks(s)
        if s > 1:
            forward(s - 1)
        arrive(s - 1)
    finish()
    if ny == 2:
        for dz in range(nz):
            for dp in range(2):
                slot = dz * 2 + dp
                source = at.rank(
                    lax.rem(at.p + dp, 2), at.chip(at.down(at.z, dz), 1 - at.y)
                )
                there = blocks.at[source]
                remote(there, there, fs.at[slot], fr.at[slot], at.across).wait_recv()
    for copy in sends + square_copies:
        copy.wait_send()
    swap.wait()
    keep.wait()


def front(ny, nt, group_size, hidden, gain, kv_pool, w_out, w_query):
    rows, width = hidden.shape
    columns = w_query.shape[1]
    nz = nt // ny
    ranks = 2 * nt
    dma = pltpu.SemaphoreType.DMA
    blocks = (ranks, kv_pool.shape[0]) + kv_pool.shape[2:]
    return pl.pallas_call(
        functools.partial(front_kernel, ny, nt, group_size),
        out_shape=(
            jax.ShapeDtypeStruct((rows, columns), jnp.float32),
            jax.ShapeDtypeStruct(blocks, kv_pool.dtype),
            jax.ShapeDtypeStruct((w_out.shape[0], w_out.shape[1] // 2), w_out.dtype),
        ),
        in_specs=[pl.BlockSpec(memory_space=pltpu.VMEM)] * 2
        + [pl.BlockSpec(memory_space=pl.ANY)] * 3,
        out_specs=(
            pl.BlockSpec(memory_space=pltpu.VMEM),
            pl.BlockSpec(memory_space=pl.ANY),
            pl.BlockSpec(memory_space=pl.ANY),
        ),
        scratch_shapes=[
            pltpu.VMEM((8, rows), jnp.float32),
            pltpu.VMEM((ranks - 1, 8, rows), jnp.float32),
            pltpu.VMEM((rows, 128), jnp.float32),
            pltpu.VMEM((rows, width), hidden.dtype),
            pltpu.VMEM((ranks, rows, width), hidden.dtype),
            pltpu.VMEM((ranks, width, columns), w_query.dtype),
        ]
        + gather_sems(ny, nz)
        + [dma((2 * nz,)), dma((2 * nz,)), dma((2 * nz,)), dma((2 * nz,)), dma, dma, dma]
        + [dma((ranks,)), dma((ranks - 1,)), dma((ranks - 1,))],
        compiler_params=pltpu.CompilerParams(
            collective_id=0, has_side_effects=True, vmem_limit_bytes=WIDE_VMEM_LIMIT
        ),
        name="front",
    )(hidden, gain, kv_pool, w_out, w_query)


def code(value, codes, scales):
    peak = jnp.maximum(jnp.max(jnp.abs(value), axis=0, keepdims=True), 1e-30)
    codes[...] = jnp.round(value * (32767.0 / peak)).astype(jnp.int32).astype(jnp.int16)
    scales[...] = jnp.broadcast_to(peak * (1.0 / 32767.0), scales.shape)


def decode(codes, scales):
    return codes[...].astype(jnp.int32).astype(jnp.float32) * scales[0:1, :]


def back_kernel(
    ny, nt, heads, w_own, w_mate, out,
    heads_mate, w_buf, y_send, y_recv, z_send, z_recv,
    y_send_scale, y_recv_scale, z_send_scale, z_recv_scale, final,
    hs, hr, w_sem, ps, pr, qs, qr, pss, psr, qss, qsr, zs, zr, ys, yr, ms, mr, ls,
):
    at = Place(ny, nt)
    nz = at.nz
    width = final.shape[1]
    half = w_mate.shape[1]

    def load(which, t):
        if which == 0:
            start = pl.multiple_of(at.p * half + t * width, width)
            src = w_own.at[:, pl.ds(start, width)]
        else:
            src = w_mate.at[:, pl.ds(pl.multiple_of(t * width, width), width)]
        return pltpu.make_async_copy(src, w_buf.at[which, t], w_sem.at[which, t])

    part = heads.shape[0] // PIECES

    def chip_of(s, y):
        return at.chip(lax.rem(at.z + 2 * nz - 1 - s, nz), y)

    def start_loads(y):
        def body(s, carry):
            t = chip_of(s, y)
            load(0, t).start()
            load(1, t).start()
            return carry

        lax.fori_loop(0, nz, body, 0)

    if ny == 2:
        start_loads(1 - at.y)
    start_loads(at.y)
    neighbours = [at.mate, at.next, at.previous] + ([at.across] if ny == 2 else [])
    meet(neighbours)
    trade = remote(heads, heads_mate, hs, hr, at.mate)
    trade.start()
    trade.wait()

    def rows_of(i):
        return pl.ds(pl.multiple_of(lax.rem(i, PIECES) * part, part), part)

    def wait_loads(y):
        def body(s, carry):
            t = chip_of(s, y)
            load(0, t).wait()
            load(1, t).wait()
            return carry

        lax.fori_loop(0, nz, body, 0)

    def term(i, y):
        t = chip_of(i // PIECES, y)
        return jnp.dot(
            heads[rows_of(i), :], w_buf[0, t], preferred_element_type=jnp.float32
        ) + jnp.dot(heads_mate[rows_of(i), :], w_buf[1, t], preferred_element_type=jnp.float32)

    def across_copies(i):
        return [
            remote(y_send.at[i], y_recv.at[i], ps.at[i], pr.at[i], at.across),
            remote(y_send_scale.at[i], y_recv_scale.at[i], pss.at[i], psr.at[i], at.across),
        ]

    def ring_copies(i):
        return [
            remote(z_send.at[i], z_recv.at[i], qs.at[i], qr.at[i], at.next),
            remote(z_send_scale.at[i], z_recv_scale.at[i], qss.at[i], qsr.at[i], at.next),
        ]

    if ny == 2:
        wait_loads(1 - at.y)

        def send_across(i, carry):
            code(term(i, 1 - at.y), y_send.at[i], y_send_scale.at[i])
            for copy in across_copies(i):
                copy.start()
            return carry

        lax.fori_loop(0, nz * PIECES, send_across, 0)
    wait_loads(at.y)

    def total(i):
        value = term(i, at.y)
        if ny == 2:
            for copy in across_copies(i):
                copy.wait_recv()
            value = value + decode(y_recv.at[i], y_recv_scale.at[i])
        return value

    def ring_received(i):
        for copy in ring_copies(i):
            copy.wait_recv()
        return decode(z_recv.at[i], z_recv_scale.at[i])

    def ring_send(i, value):
        code(value, z_send.at[i], z_send_scale.at[i])
        for copy in ring_copies(i):
            copy.start()

    def ring_first(i, carry):
        ring_send(i, total(i))
        return carry

    lax.fori_loop(0, PIECES, ring_first, 0)

    def ring_step(i, carry):
        value = total(i)
        ring_send(i, value + ring_received(i - PIECES))
        return carry

    lax.fori_loop(PIECES, (nz - 1) * PIECES, ring_step, 0)

    def block_of(rank):
        return out.at[:, pl.ds(pl.multiple_of(rank * width, width), width)]

    step, arrive, finish = gather_blocks(
        at, final, block_of, (zs, zr, ys, yr, ms, mr, ls), keep_last=True
    )
    for h in range(PIECES):
        i = (nz - 1) * PIECES + h
        value = total(i)
        final[h * part : (h + 1) * part, :] = (value + ring_received(i - PIECES)).astype(
            final.dtype
        )
        step(0, (h,))
    for s in range(1, nz + 1):
        step(s)
    for s in range(nz):
        arrive(s)
    finish()

    def sent(i, carry):
        if ny == 2:
            for copy in across_copies(i):
                copy.wait_send()
        return carry

    lax.fori_loop(0, nz * PIECES, sent, 0)

    def ring_sent(s, carry):
        for copy in ring_copies(s):
            copy.wait_send()
        return carry

    lax.fori_loop(0, (nz - 1) * PIECES, ring_sent, 0)


def back(ny, nt, heads, w_out, w_mate):
    rows, depth = heads.shape
    columns = w_out.shape[1]
    nz = nt // ny
    width = columns // (2 * nt)
    dma = pltpu.SemaphoreType.DMA
    f32 = jnp.float32
    return pl.pallas_call(
        functools.partial(back_kernel, ny, nt),
        out_shape=jax.ShapeDtypeStruct((rows, columns), jnp.bfloat16),
        in_specs=[
            pl.BlockSpec(memory_space=pltpu.VMEM),
            pl.BlockSpec(memory_space=pl.ANY),
            pl.BlockSpec(memory_space=pl.ANY),
        ],
        out_specs=pl.BlockSpec(memory_space=pl.ANY),
        scratch_shapes=[
            pltpu.VMEM((rows, depth), heads.dtype),
            pltpu.VMEM((2, nt, depth, width), w_out.dtype),
            pltpu.VMEM((nz * PIECES, rows // PIECES, width), jnp.int16),
            pltpu.VMEM((nz * PIECES, rows // PIECES, width), jnp.int16),
            pltpu.VMEM(((nz - 1) * PIECES, rows // PIECES, width), jnp.int16),
            pltpu.VMEM(((nz - 1) * PIECES, rows // PIECES, width), jnp.int16),
            pltpu.VMEM((nz * PIECES, 8, width), f32),
            pltpu.VMEM((nz * PIECES, 8, width), f32),
            pltpu.VMEM(((nz - 1) * PIECES, 8, width), f32),
            pltpu.VMEM(((nz - 1) * PIECES, 8, width), f32),
            pltpu.VMEM((rows, width), jnp.bfloat16),
            dma,
            dma,
            dma((2, nt)),
            dma((nz * PIECES,)),
            dma((nz * PIECES,)),
            dma((nz * PIECES,)),
            dma((nz * PIECES,)),
            dma((nz * PIECES,)),
            dma((nz * PIECES,)),
            dma((nz * PIECES,)),
            dma((nz * PIECES,)),
        ]
        + gather_sems(ny, nz),
        compiler_params=pltpu.CompilerParams(
            collective_id=1, has_side_effects=True, vmem_limit_bytes=VMEM_LIMIT
        ),
        name="back",
    )(heads, w_out, w_mate)


def attention_kernel(
    table, lengths, head, raw, depth_down, depth_along, frequency, draft_kv, blocks, out, keys, values, sems
):
    request = pl.program_id(0)
    requests, context, head_dim = keys.shape
    block_len = blocks.shape[2]
    listed = context // block_len

    def copies(r, j):
        here = pl.ds(pl.multiple_of(j * block_len, block_len), block_len)
        block = table[r, j]
        return [
            pltpu.make_async_copy(blocks.at[block, 0], keys.at[r, here, :], sems.at[0, r, j]),
            pltpu.make_async_copy(blocks.at[block, 1], values.at[r, here, :], sems.at[1, r, j]),
        ]

    @pl.when(request == 0)
    def _():
        def start(i, carry):
            for copy in copies(i // listed, lax.rem(i, listed)):
                copy.start()
            return carry

        lax.fori_loop(0, requests * listed, start, 0)

    def arrived(j, carry):
        for copy in copies(request, j):
            copy.wait()
        return carry

    lax.fori_loop(0, listed, arrived, 0)
    both = (((1,), (1,)), ((), ()))
    f32 = jnp.float32
    valid = lax.broadcasted_iota(jnp.int32, (1, context), 1) < lengths[request]
    drafts = raw.shape[0]
    angles = (lengths[request] + depth_down[...]).astype(f32) * frequency[...]
    cosine = jnp.cos(angles)
    sine = jnp.sin(angles)
    sine = jnp.where(
        lax.broadcasted_iota(jnp.int32, (1, head_dim), 1) < head_dim // 2, -sine, sine
    )
    square = (drafts, drafts)
    draft_valid = (depth_along[0] < depth_down[...]) | (
        lax.broadcasted_iota(jnp.int32, square, 0) == lax.broadcasted_iota(jnp.int32, square, 1)
    )
    draft_k = draft_kv[:, 0, :]
    draft_v = draft_kv[:, 1, :]
    heads = raw.shape[1] // head_dim
    queries = []
    for h in range(heads):
        query = raw[:, h * head_dim : (h + 1) * head_dim]
        swapped = jnp.concatenate(
            [query[:, head_dim // 2 :], query[:, : head_dim // 2]], axis=1
        )
        query = query * cosine + swapped * sine
        queries.append((query * head_dim ** (-0.5)).astype(jnp.bfloat16))
    query = jnp.concatenate(queries, axis=0)
    cache = lax.dot_general(query, keys[request], both, preferred_element_type=f32)
    cache = jnp.where(valid, cache, -jnp.inf)
    draft = lax.dot_general(query, draft_k, both, preferred_element_type=f32)
    draft = jnp.concatenate(
        [
            jnp.where(draft_valid, draft[h * drafts : (h + 1) * drafts, :], -jnp.inf)
            for h in range(heads)
        ],
        axis=0,
    )
    peak = jnp.maximum(
        jnp.max(cache, axis=-1, keepdims=True), jnp.max(draft, axis=-1, keepdims=True)
    )
    cache = jnp.exp(cache - peak)
    draft = jnp.exp(draft - peak)
    share = 1.0 / (
        jnp.sum(cache, axis=-1, keepdims=True) + jnp.sum(draft, axis=-1, keepdims=True)
    )
    cache = (cache * share).astype(jnp.bfloat16)
    draft = (draft * share).astype(jnp.bfloat16)
    rows = jnp.dot(cache, values[request], preferred_element_type=f32)
    rows = rows + jnp.dot(draft, draft_v, preferred_element_type=f32)
    for h in range(heads):
        out[:, h * head_dim : (h + 1) * head_dim] = rows[
            h * drafts : (h + 1) * drafts, :
        ].astype(out.dtype)


def attention(raw, depth, frequency, draft_kv, blocks, table, lengths, head):
    rows, columns = raw.shape
    requests, listed = table.shape
    drafts = rows // requests
    block_len, head_dim = blocks.shape[2:]
    context = listed * block_len

    def by_rows(width):
        return pl.BlockSpec((drafts, width), lambda r, *_: (r, 0))

    return pl.pallas_call(
        attention_kernel,
        out_shape=jax.ShapeDtypeStruct((rows, columns), jnp.bfloat16),
        grid_spec=pltpu.PrefetchScalarGridSpec(
            num_scalar_prefetch=3,
            grid=(requests,),
            in_specs=[
                by_rows(columns),
                by_rows(1),
                pl.BlockSpec((1, 1, drafts), lambda r, *_: (r, 0, 0)),
                pl.BlockSpec((1, head_dim), lambda r, *_: (0, 0)),
                pl.BlockSpec((drafts, 2, head_dim), lambda r, table, lengths, head: (r, 0, head[0])),
                pl.BlockSpec(memory_space=pl.ANY),
            ],
            out_specs=by_rows(columns),
            scratch_shapes=[
                pltpu.VMEM((requests, context, head_dim), blocks.dtype),
                pltpu.VMEM((requests, context, head_dim), blocks.dtype),
                pltpu.SemaphoreType.DMA((2, requests, listed)),
            ],
        ),
        compiler_params=pltpu.CompilerParams(
            dimension_semantics=("arbitrary",), vmem_limit_bytes=WIDE_VMEM_LIMIT
        ),
        name="mid",
    )(
        table, lengths, head, raw, depth.reshape(rows, 1), depth[:, None, :], frequency,
        draft_kv, blocks,
    )


def shards(
    hidden, norm_gain, w_query, w_out, kv_pool, draft_kv, block_table, cached_len, draft_pos
):
    nt = lax.axis_size("tensor")
    ny = 2 if nt == 8 else 1
    devices = lax.axis_size(("pool", "tensor"))
    my_rank = lax.axis_index(("pool", "tensor"))
    kv_heads = kv_pool.shape[1]
    block_len = kv_pool.shape[3]
    head_dim = kv_pool.shape[4]
    group_size = devices // kv_heads
    own_head = my_rank // group_size
    gain = norm_gain.reshape(1, -1)
    raw_queries, arrived, w_mate = front(
        ny, nt, group_size, hidden, gain, kv_pool, w_out, w_query
    )
    half = np.arange(head_dim // 2, dtype=np.float64)
    frequency = np.tile(500000.0 ** (-2.0 * half / head_dim), 2).astype(np.float32)
    blocks = arrived.reshape(-1, 2, block_len, head_dim)
    heads_out = attention(
        raw_queries, draft_pos, jnp.asarray(frequency)[None, :], draft_kv, blocks,
        block_table, cached_len, jnp.reshape(own_head, (1,)),
    )
    return back(ny, nt, heads_out, w_out, w_mate)


def solution(mesh):
    placed = (
        P("groups", ("pool", "tensor")),
        P(),
        P(None, ("pool", "tensor")),
        P(("pool", "tensor"), None),
        P(("groups", "pool", "tensor"), None, None, None, None),
        P("groups", None, None),
        P("groups", None),
        P("groups"),
        P("groups", None),
    )
    return jax.shard_map(
        shards, mesh=mesh, in_specs=placed, out_specs=P("groups", None), check_vma=False
    )
```

```python
import functools

import jax
import jax.numpy as jnp
import numpy as np
from jax import lax
from jax.experimental import pallas as pl
from jax.experimental.pallas import tpu as pltpu
from jax.sharding import PartitionSpec as P

VMEM_LIMIT = 40 * 1024 * 1024
WIDE_VMEM_LIMIT = 56 * 1024 * 1024
PIECES = 2


class Place:
    def __init__(self, ny, nt):
        self.ny, self.nz, self.nt = ny, nt // ny, nt
        self.p = lax.axis_index("pool")
        self.t = lax.axis_index("tensor")
        self.y = lax.rem(self.t, ny)
        self.z = self.t // ny

    def chip(self, z, y):
        return z * self.ny + y

    def up(self, z, by):
        return lax.rem(z + by, self.nz)

    def down(self, z, by):
        return lax.rem(z + self.nz - by, self.nz)

    def rank(self, p, t):
        return p * self.nt + t

    @property
    def mate(self):
        return {"pool": 1 - self.p, "tensor": self.t}

    @property
    def across(self):
        return {"pool": self.p, "tensor": self.chip(self.z, 1 - self.y)}

    @property
    def next(self):
        return {"pool": self.p, "tensor": self.chip(self.up(self.z, 1), self.y)}

    @property
    def previous(self):
        return {"pool": self.p, "tensor": self.chip(self.down(self.z, 1), self.y)}


def remote(src, dst, send, recv, device):
    return pltpu.make_async_remote_copy(
        src_ref=src,
        dst_ref=dst,
        send_sem=send,
        recv_sem=recv,
        device_id=device,
        device_id_type=pl.DeviceIdType.MESH,
    )


def meet(devices):
    barrier = pltpu.get_barrier_semaphore()
    for device in devices:
        pl.semaphore_signal(barrier, inc=1, device_id=device, device_id_type=pl.DeviceIdType.MESH)
    pl.semaphore_wait(barrier, len(devices))


def gather_blocks(at, own, block_of, sems, use=None, keep_last=False):
    zs, zr, ys, yr, ms, mr, ls = sems
    nz, ny = at.nz, at.ny
    part = own.shape[0] // PIECES

    def rows(ref, h):
        return ref.at[pl.ds(h * part, part), :]

    def block(p, z, y, h):
        return rows(block_of(at.rank(p, at.chip(z, y))), h)

    if keep_last:
        keep = pltpu.make_async_copy(own, block_of(at.rank(at.p, at.t)), ls)
    started = []

    def send(src, dst, send_sem, recv_sem, device):
        started.append(remote(src, dst, send_sem, recv_sem, device))
        started[-1].start()

    def ring(s, h):
        z = at.down(at.z, s)
        here = block(at.p, z, at.y, h)
        src = rows(own, h) if s == 0 else here
        if s > 0:
            remote(here, here, zs.at[s - 1, h], zr.at[s - 1, h], at.previous).wait_recv()
        if s < nz - 1:
            send(src, here, zs.at[s, h], zr.at[s, h], at.next)
        if ny == 2:
            send(src, here, ys.at[s, h], yr.at[s, h], at.across)
        send(src, here, ms.at[s, h], mr.at[s, h], at.mate)

    def from_across(s, h):
        if ny == 2:
            there = block(at.p, at.down(at.z, s), 1 - at.y, h)
            remote(there, there, ys.at[s, h], yr.at[s, h], at.across).wait_recv()
            send(there, there, ms.at[nz + s, h], mr.at[nz + s, h], at.mate)

    def step(s, pieces=range(PIECES)):
        for h in pieces:
            if s < nz:
                ring(s, h)
            if s > 0:
                from_across(s - 1, h)
            if keep_last and s == 0 and h == PIECES - 1:
                keep.start()

    def arrive(s):
        z = at.down(at.z, s)
        for y_at in range(ny):
            y = at.y if y_at == 0 else 1 - at.y
            slot = s + y_at * nz
            if use is not None and s + y_at > 0:
                use(at.rank(at.p, at.chip(z, y)))
            for h in range(PIECES):
                there = block(1 - at.p, z, y, h)
                remote(there, there, ms.at[slot, h], mr.at[slot, h], at.mate).wait_recv()
            if use is not None:
                use(at.rank(1 - at.p, at.chip(z, y)))

    def finish():
        for copy in started:
            copy.wait_send()
        if keep_last:
            keep.wait()

    return step, arrive, finish


def gather_sems(ny, nz):
    dma = pltpu.SemaphoreType.DMA
    once, twice = dma((nz, PIECES)), dma((2 * nz, PIECES))
    return [once, once, once, once, twice, twice, dma]


def front_kernel(
    ny, nt, group_size, hidden, gain, kv, w_out, w_query, raw, blocks, w_mate,
    squares, squares_all, scales, normed, gathered, w_buf,
    zs, zr, ys, yr, ms, mr, ls, ks, kr, fs, fr, ws, wr, bs, w_sem, ss, sr,
):
    at = Place(ny, nt)
    nz = at.nz
    ranks = 2 * nt
    width = hidden.shape[1]

    def load(rank):
        start = pl.multiple_of(rank * width, width)
        return pltpu.make_async_copy(
            w_query.at[pl.ds(start, width), :], w_buf.at[rank], w_sem.at[rank]
        )

    def start_load(rank, carry):
        load(rank).start()
        return carry

    lax.fori_loop(0, ranks, start_load, 0)
    others = []
    for dt in range(nt):
        for dp in range(2):
            if dt + dp > 0:
                others.append({"pool": lax.rem(at.p + dp, 2), "tensor": lax.rem(at.t + dt, nt)})
    meet(others)
    me = at.rank(at.p, at.t)
    step, arrive, finish = gather_blocks(
        at, hidden, lambda rank: gathered.at[rank], (zs, zr, ys, yr, ms, mr, ls),
        lambda rank: use(rank),
    )
    step(0)

    wide = hidden[...].astype(jnp.float32)
    squares[...] = lax.dot_general(
        jnp.ones((8, width), jnp.float32), wide * wide, (((1,), (1,)), ((), ())),
        precision=lax.Precision.HIGHEST, preferred_element_type=jnp.float32,
    )
    square_copies = [
        remote(squares, squares_all.at[i], ss.at[i], sr.at[i], device)
        for i, device in enumerate(others)
    ]
    for copy in square_copies:
        copy.start()

    def head_of(p, t):
        return at.rank(p, t) // group_size

    keep = pltpu.make_async_copy(kv.at[:, head_of(at.p, at.t)], blocks.at[me], bs)
    keep.start()
    half = w_mate.shape[1]
    swap = remote(
        w_out.at[:, pl.ds(pl.multiple_of((1 - at.p) * half, half), half)],
        w_mate, ws, wr, at.mate,
    )
    sends = []

    def send_blocks(dz):
        for dp in range(2):
            if dz + dp > 0:
                device = {
                    "pool": lax.rem(at.p + dp, 2),
                    "tensor": at.chip(at.up(at.z, dz), at.y),
                }
                slot = dz * 2 + dp
                head = head_of(device["pool"], device["tensor"])
                sends.append(remote(kv.at[:, head], blocks.at[me], ks.at[slot], kr.at[slot], device))
                sends[-1].start()

    send_blocks(0)

    def use(rank):
        load(rank).wait()
        start = pl.multiple_of(rank * width, width)
        for c in range(width // 128):
            lanes = slice(c * 128, (c + 1) * 128)
            features = pl.ds(pl.multiple_of(start + c * 128, 128), 128)
            normed[:, lanes] = (
                gathered[rank, :, lanes].astype(jnp.float32) * scales[...] * gain[:, features]
            ).astype(normed.dtype)
        raw[...] += jnp.dot(normed[...], w_buf[rank], preferred_element_type=jnp.float32)

    def sum_squares():
        total = squares[...]
        for i, copy in enumerate(square_copies):
            copy.wait_recv()
            total = total + squares_all[i]
        scale = lax.rsqrt(total * (1.0 / (width * ranks)) + 1e-05)
        scales[...] = jnp.transpose(jnp.concatenate([scale] * 16, axis=0))

    def block_from(dz, dp):
        return at.rank(lax.rem(at.p + dp, 2), at.chip(at.down(at.z, dz), at.y))

    def forward(dz):
        for dp in range(2):
            slot = dz * 2 + dp
            here = blocks.at[block_from(dz, dp)]
            src = here
            if slot == 0:
                src = kv.at[:, head_of(at.p, at.t)]
            else:
                remote(here, here, ks.at[slot], kr.at[slot], at.mate).wait_recv()
            if ny == 2:
                sends.append(remote(src, here, fs.at[slot], fr.at[slot], at.across))
                sends[-1].start()

    forward(0)
    swap.start()
    gathered[me] = hidden[...]
    raw[...] = jnp.zeros_like(raw)
    sum_squares()
    use(me)
    for s in range(1, nz + 1):
        step(s)
        if s < nz:
            send_blocks(s)
        if s > 1:
            forward(s - 1)
        arrive(s - 1)
    finish()
    if ny == 2:
        for dz in range(nz):
            for dp in range(2):
                slot = dz * 2 + dp
                source = at.rank(
                    lax.rem(at.p + dp, 2), at.chip(at.down(at.z, dz), 1 - at.y)
                )
                there = blocks.at[source]
                remote(there, there, fs.at[slot], fr.at[slot], at.across).wait_recv()
    for copy in sends + square_copies:
        copy.wait_send()
    swap.wait()
    keep.wait()


def front(ny, nt, group_size, hidden, gain, kv_pool, w_out, w_query):
    rows, width = hidden.shape
    columns = w_query.shape[1]
    nz = nt // ny
    ranks = 2 * nt
    dma = pltpu.SemaphoreType.DMA
    blocks = (ranks, kv_pool.shape[0]) + kv_pool.shape[2:]
    return pl.pallas_call(
        functools.partial(front_kernel, ny, nt, group_size),
        out_shape=(
            jax.ShapeDtypeStruct((rows, columns), jnp.float32),
            jax.ShapeDtypeStruct(blocks, kv_pool.dtype),
            jax.ShapeDtypeStruct((w_out.shape[0], w_out.shape[1] // 2), w_out.dtype),
        ),
        in_specs=[pl.BlockSpec(memory_space=pltpu.VMEM)] * 2
        + [pl.BlockSpec(memory_space=pl.ANY)] * 3,
        out_specs=(
            pl.BlockSpec(memory_space=pltpu.VMEM),
            pl.BlockSpec(memory_space=pl.ANY),
            pl.BlockSpec(memory_space=pl.ANY),
        ),
        scratch_shapes=[
            pltpu.VMEM((8, rows), jnp.float32),
            pltpu.VMEM((ranks - 1, 8, rows), jnp.float32),
            pltpu.VMEM((rows, 128), jnp.float32),
            pltpu.VMEM((rows, width), hidden.dtype),
            pltpu.VMEM((ranks, rows, width), hidden.dtype),
            pltpu.VMEM((ranks, width, columns), w_query.dtype),
        ]
        + gather_sems(ny, nz)
        + [dma((2 * nz,)), dma((2 * nz,)), dma((2 * nz,)), dma((2 * nz,)), dma, dma, dma]
        + [dma((ranks,)), dma((ranks - 1,)), dma((ranks - 1,))],
        compiler_params=pltpu.CompilerParams(
            collective_id=0, has_side_effects=True, vmem_limit_bytes=WIDE_VMEM_LIMIT
        ),
        name="front",
    )(hidden, gain, kv_pool, w_out, w_query)


def code(value, codes, scales):
    peak = jnp.maximum(jnp.max(jnp.abs(value), axis=0, keepdims=True), 1e-30)
    codes[...] = jnp.round(value * (32767.0 / peak)).astype(jnp.int32).astype(jnp.int16)
    scales[...] = jnp.broadcast_to(peak * (1.0 / 32767.0), scales.shape)


def decode(codes, scales):
    return codes[...].astype(jnp.int32).astype(jnp.float32) * scales[0:1, :]


def back_kernel(
    ny, nt, heads, w_own, w_mate, out,
    heads_mate, w_buf, y_send, y_recv, z_send, z_recv,
    y_send_scale, y_recv_scale, z_send_scale, z_recv_scale, final,
    hs, hr, w_sem, ps, pr, qs, qr, pss, psr, qss, qsr, zs, zr, ys, yr, ms, mr, ls,
):
    at = Place(ny, nt)
    nz = at.nz
    width = final.shape[1]
    half = w_mate.shape[1]

    def load(which, t):
        if which == 0:
            start = pl.multiple_of(at.p * half + t * width, width)
            src = w_own.at[:, pl.ds(start, width)]
        else:
            src = w_mate.at[:, pl.ds(pl.multiple_of(t * width, width), width)]
        return pltpu.make_async_copy(src, w_buf.at[which, t], w_sem.at[which, t])

    part = heads.shape[0] // PIECES

    def chip_of(s, y):
        return at.chip(lax.rem(at.z + 2 * nz - 1 - s, nz), y)

    def start_loads(y):
        def body(s, carry):
            t = chip_of(s, y)
            load(0, t).start()
            load(1, t).start()
            return carry

        lax.fori_loop(0, nz, body, 0)

    if ny == 2:
        start_loads(1 - at.y)
    start_loads(at.y)
    neighbours = [at.mate, at.next, at.previous] + ([at.across] if ny == 2 else [])
    meet(neighbours)
    trade = remote(heads, heads_mate, hs, hr, at.mate)
    trade.start()
    trade.wait()

    def rows_of(i):
        return pl.ds(pl.multiple_of(lax.rem(i, PIECES) * part, part), part)

    def wait_loads(y):
        def body(s, carry):
            t = chip_of(s, y)
            load(0, t).wait()
            load(1, t).wait()
            return carry

        lax.fori_loop(0, nz, body, 0)

    def term(i, y):
        t = chip_of(i // PIECES, y)
        return jnp.dot(
            heads[rows_of(i), :], w_buf[0, t], preferred_element_type=jnp.float32
        ) + jnp.dot(heads_mate[rows_of(i), :], w_buf[1, t], preferred_element_type=jnp.float32)

    def across_copies(i):
        return [
            remote(y_send.at[i], y_recv.at[i], ps.at[i], pr.at[i], at.across),
            remote(y_send_scale.at[i], y_recv_scale.at[i], pss.at[i], psr.at[i], at.across),
        ]

    def ring_copies(i):
        return [
            remote(z_send.at[i], z_recv.at[i], qs.at[i], qr.at[i], at.next),
            remote(z_send_scale.at[i], z_recv_scale.at[i], qss.at[i], qsr.at[i], at.next),
        ]

    if ny == 2:
        wait_loads(1 - at.y)

        def send_across(i, carry):
            code(term(i, 1 - at.y), y_send.at[i], y_send_scale.at[i])
            for copy in across_copies(i):
                copy.start()
            return carry

        lax.fori_loop(0, nz * PIECES, send_across, 0)
    wait_loads(at.y)

    def total(i):
        value = term(i, at.y)
        if ny == 2:
            for copy in across_copies(i):
                copy.wait_recv()
            value = value + decode(y_recv.at[i], y_recv_scale.at[i])
        return value

    def ring_received(i):
        for copy in ring_copies(i):
            copy.wait_recv()
        return decode(z_recv.at[i], z_recv_scale.at[i])

    def ring_send(i, value):
        code(value, z_send.at[i], z_send_scale.at[i])
        for copy in ring_copies(i):
            copy.start()

    def ring_first(i, carry):
        ring_send(i, total(i))
        return carry

    lax.fori_loop(0, PIECES, ring_first, 0)

    def ring_step(i, carry):
        value = total(i)
        ring_send(i, value + ring_received(i - PIECES))
        return carry

    lax.fori_loop(PIECES, (nz - 1) * PIECES, ring_step, 0)

    def block_of(rank):
        return out.at[:, pl.ds(pl.multiple_of(rank * width, width), width)]

    step, arrive, finish = gather_blocks(
        at, final, block_of, (zs, zr, ys, yr, ms, mr, ls), keep_last=True
    )
    for h in range(PIECES):
        i = (nz - 1) * PIECES + h
        value = total(i)
        final[h * part : (h + 1) * part, :] = (value + ring_received(i - PIECES)).astype(
            final.dtype
        )
        step(0, (h,))
    for s in range(1, nz + 1):
        step(s)
    for s in range(nz):
        arrive(s)
    finish()

    def sent(i, carry):
        if ny == 2:
            for copy in across_copies(i):
                copy.wait_send()
        return carry

    lax.fori_loop(0, nz * PIECES, sent, 0)

    def ring_sent(s, carry):
        for copy in ring_copies(s):
            copy.wait_send()
        return carry

    lax.fori_loop(0, (nz - 1) * PIECES, ring_sent, 0)


def back(ny, nt, heads, w_out, w_mate):
    rows, depth = heads.shape
    columns = w_out.shape[1]
    nz = nt // ny
    width = columns // (2 * nt)
    dma = pltpu.SemaphoreType.DMA
    f32 = jnp.float32
    return pl.pallas_call(
        functools.partial(back_kernel, ny, nt),
        out_shape=jax.ShapeDtypeStruct((rows, columns), jnp.bfloat16),
        in_specs=[
            pl.BlockSpec(memory_space=pltpu.VMEM),
            pl.BlockSpec(memory_space=pl.ANY),
            pl.BlockSpec(memory_space=pl.ANY),
        ],
        out_specs=pl.BlockSpec(memory_space=pl.ANY),
        scratch_shapes=[
            pltpu.VMEM((rows, depth), heads.dtype),
            pltpu.VMEM((2, nt, depth, width), w_out.dtype),
            pltpu.VMEM((nz * PIECES, rows // PIECES, width), jnp.int16),
            pltpu.VMEM((nz * PIECES, rows // PIECES, width), jnp.int16),
            pltpu.VMEM(((nz - 1) * PIECES, rows // PIECES, width), jnp.int16),
            pltpu.VMEM(((nz - 1) * PIECES, rows // PIECES, width), jnp.int16),
            pltpu.VMEM((nz * PIECES, 8, width), f32),
            pltpu.VMEM((nz * PIECES, 8, width), f32),
            pltpu.VMEM(((nz - 1) * PIECES, 8, width), f32),
            pltpu.VMEM(((nz - 1) * PIECES, 8, width), f32),
            pltpu.VMEM((rows, width), jnp.bfloat16),
            dma,
            dma,
            dma((2, nt)),
            dma((nz * PIECES,)),
            dma((nz * PIECES,)),
            dma((nz * PIECES,)),
            dma((nz * PIECES,)),
            dma((nz * PIECES,)),
            dma((nz * PIECES,)),
            dma((nz * PIECES,)),
            dma((nz * PIECES,)),
        ]
        + gather_sems(ny, nz),
        compiler_params=pltpu.CompilerParams(
            collective_id=1, has_side_effects=True, vmem_limit_bytes=VMEM_LIMIT
        ),
        name="back",
    )(heads, w_out, w_mate)


def attention_kernel(
    table, lengths, head, raw, depth_down, depth_along, frequency, draft_kv, blocks, out, keys, values, sems
):
    request = pl.program_id(0)
    requests, context, head_dim = keys.shape
    block_len = blocks.shape[2]
    listed = context // block_len

    def copies(r, j):
        here = pl.ds(pl.multiple_of(j * block_len, block_len), block_len)
        block = table[r, j]
        return [
            pltpu.make_async_copy(blocks.at[block, 0], keys.at[r, here, :], sems.at[0, r, j]),
            pltpu.make_async_copy(blocks.at[block, 1], values.at[r, here, :], sems.at[1, r, j]),
        ]

    @pl.when(request == 0)
    def _():
        def start(i, carry):
            for copy in copies(i // listed, lax.rem(i, listed)):
                copy.start()
            return carry

        lax.fori_loop(0, requests * listed, start, 0)

    def arrived(j, carry):
        for copy in copies(request, j):
            copy.wait()
        return carry

    lax.fori_loop(0, listed, arrived, 0)
    both = (((1,), (1,)), ((), ()))
    f32 = jnp.float32
    valid = lax.broadcasted_iota(jnp.int32, (1, context), 1) < lengths[request]
    drafts = raw.shape[0]
    angles = (lengths[request] + depth_down[...]).astype(f32) * frequency[...]
    cosine = jnp.cos(angles)
    sine = jnp.sin(angles)
    sine = jnp.where(
        lax.broadcasted_iota(jnp.int32, (1, head_dim), 1) < head_dim // 2, -sine, sine
    )
    square = (drafts, drafts)
    draft_valid = (depth_along[0] < depth_down[...]) | (
        lax.broadcasted_iota(jnp.int32, square, 0) == lax.broadcasted_iota(jnp.int32, square, 1)
    )
    draft_k = draft_kv[:, 0, :]
    draft_v = draft_kv[:, 1, :]
    heads = raw.shape[1] // head_dim
    queries = []
    for h in range(heads):
        query = raw[:, h * head_dim : (h + 1) * head_dim]
        swapped = jnp.concatenate(
            [query[:, head_dim // 2 :], query[:, : head_dim // 2]], axis=1
        )
        query = query * cosine + swapped * sine
        queries.append((query * head_dim ** (-0.5)).astype(jnp.bfloat16))
    query = jnp.concatenate(queries, axis=0)
    cache = lax.dot_general(query, keys[request], both, preferred_element_type=f32)
    cache = jnp.where(valid, cache, -jnp.inf)
    draft = lax.dot_general(query, draft_k, both, preferred_element_type=f32)
    draft = jnp.concatenate(
        [
            jnp.where(draft_valid, draft[h * drafts : (h + 1) * drafts, :], -jnp.inf)
            for h in range(heads)
        ],
        axis=0,
    )
    peak = jnp.maximum(
        jnp.max(cache, axis=-1, keepdims=True), jnp.max(draft, axis=-1, keepdims=True)
    )
    cache = jnp.exp(cache - peak)
    draft = jnp.exp(draft - peak)
    share = 1.0 / (
        jnp.sum(cache, axis=-1, keepdims=True) + jnp.sum(draft, axis=-1, keepdims=True)
    )
    cache = (cache * share).astype(jnp.bfloat16)
    draft = (draft * share).astype(jnp.bfloat16)
    rows = jnp.dot(cache, values[request], preferred_element_type=f32)
    rows = rows + jnp.dot(draft, draft_v, preferred_element_type=f32)
    for h in range(heads):
        out[:, h * head_dim : (h + 1) * head_dim] = rows[
            h * drafts : (h + 1) * drafts, :
        ].astype(out.dtype)


def attention(raw, depth, frequency, draft_kv, blocks, table, lengths, head):
    rows, columns = raw.shape
    requests, listed = table.shape
    drafts = rows // requests
    block_len, head_dim = blocks.shape[2:]
    context = listed * block_len

    def by_rows(width):
        return pl.BlockSpec((drafts, width), lambda r, *_: (r, 0))

    return pl.pallas_call(
        attention_kernel,
        out_shape=jax.ShapeDtypeStruct((rows, columns), jnp.bfloat16),
        grid_spec=pltpu.PrefetchScalarGridSpec(
            num_scalar_prefetch=3,
            grid=(requests,),
            in_specs=[
                by_rows(columns),
                by_rows(1),
                pl.BlockSpec((1, 1, drafts), lambda r, *_: (r, 0, 0)),
                pl.BlockSpec((1, head_dim), lambda r, *_: (0, 0)),
                pl.BlockSpec((drafts, 2, head_dim), lambda r, table, lengths, head: (r, 0, head[0])),
                pl.BlockSpec(memory_space=pl.ANY),
            ],
            out_specs=by_rows(columns),
            scratch_shapes=[
                pltpu.VMEM((requests, context, head_dim), blocks.dtype),
                pltpu.VMEM((requests, context, head_dim), blocks.dtype),
                pltpu.SemaphoreType.DMA((2, requests, listed)),
            ],
        ),
        compiler_params=pltpu.CompilerParams(
            dimension_semantics=("arbitrary",), vmem_limit_bytes=WIDE_VMEM_LIMIT
        ),
        name="mid",
    )(
        table, lengths, head, raw, depth.reshape(rows, 1), depth[:, None, :], frequency,
        draft_kv, blocks,
    )


def shards(
    hidden, norm_gain, w_query, w_out, kv_pool, draft_kv, block_table, cached_len, draft_pos
):
    nt = lax.axis_size("tensor")
    ny = 2 if nt == 8 else 1
    devices = lax.axis_size(("pool", "tensor"))
    my_rank = lax.axis_index(("pool", "tensor"))
    kv_heads = kv_pool.shape[1]
    block_len = kv_pool.shape[3]
    head_dim = kv_pool.shape[4]
    group_size = devices // kv_heads
    own_head = my_rank // group_size
    gain = norm_gain.reshape(1, -1)
    raw_queries, arrived, w_mate = front(
        ny, nt, group_size, hidden, gain, kv_pool, w_out, w_query
    )
    half = np.arange(head_dim // 2, dtype=np.float64)
    frequency = np.tile(500000.0 ** (-2.0 * half / head_dim), 2).astype(np.float32)
    blocks = arrived.reshape(-1, 2, block_len, head_dim)
    heads_out = attention(
        raw_queries, draft_pos, jnp.asarray(frequency)[None, :], draft_kv, blocks,
        block_table, cached_len, jnp.reshape(own_head, (1,)),
    )
    return back(ny, nt, heads_out, w_out, w_mate)


def solution(mesh):
    placed = (
        P("groups", ("pool", "tensor")),
        P(),
        P(None, ("pool", "tensor")),
        P(("pool", "tensor"), None),
        P(("groups", "pool", "tensor"), None, None, None, None),
        P("groups", None, None),
        P("groups", None),
        P("groups"),
        P("groups", None),
    )
    return jax.shard_map(
        shards, mesh=mesh, in_specs=placed, out_specs=P("groups", None), check_vma=False
    )
```
